128 devices in a mesh: dp: 128 (over y, z, x, core).
Axes of the slice: x: 4, y: 4, z: 4, core: 2. Of those that a mesh axis runs over, the one named last changes fastest.
Arguments:
- images: bfloat16 [98304, 1152], P('dp'), may hold values from -0.19921875 to 0.19921875
- texts: bfloat16 [98304, 1152], P('dp'), may hold values from -0.19921875 to 0.19921875
- pair_ids: int32 [98304], P('dp'), may hold values from 0 to 191
- log_scale: float32 [1], replicated, may hold values from 1 to 2.3
- bias: float32 [1], replicated, may hold values from -6 to -2
Outputs:
- grad_images: float32 [98304, 1152], P('dp')
- grad_texts: float32 [98304, 1152], P('dp')
The draws below stay inside these ranges and needn't reach their ends.
All inputs are finite; a program needn't handle non-finite values.
Results may differ from the reference program's by a relative error of at most 0.0042.
Values may be sent and summed in bfloat16 or wider, within the bound.
No kernel may reach another device: no remote copies, remote signals or barrier semaphores. Data moves between devices by JAX's collectives and lax.ppermute only.
A program may use at most 128 MiB of HBM per device.

```python
import jax
import jax.numpy as jnp
from jax import lax

D = 1152
ROWS = 768
STEPS = 4
GROUPS = 192
TOTAL = 98304


def with_ends(drawn, stream_key, smallest, top_value):
    index_at = [jax.random.randint(jax.random.fold_in(stream_key, axis), (), 0, length) for axis, length in enumerate(drawn.shape)]
    main_axis = drawn.shape.index(max(drawn.shape))
    beside = index_at[:main_axis] + [(index_at[main_axis] + 1) % drawn.shape[main_axis]] + index_at[main_axis + 1:]
    return drawn.at[tuple(index_at)].set(smallest).at[tuple(beside)].set(top_value)


def steps_of(stream_key, extent, split, smallest, high):
    def one(dim, shards_of):
        steps = jax.random.uniform(jax.random.fold_in(jax.random.fold_in(stream_key, 6), dim), (shards_of,), jnp.float32, smallest / len(split), high / len(split))
        return jnp.repeat(jnp.exp(steps), extent[dim] // shards_of).reshape((-1,) + (1,) * (len(extent) - dim - 1))

    gain = one(*split[0])
    for cut in split[1:]:
        gain = gain * one(*cut)
    return gain


def noise(own_key, shape, width, most, cuts=(), held_as=jnp.bfloat16):
    level = steps_of(own_key, shape, cuts, -0.22, 0.18) if cuts else 1.0
    result = jax.random.normal(own_key, shape, jnp.float32) * width * level
    return jnp.minimum(jnp.maximum(result, -most), most).astype(held_as)


def setup_inputs(seed: int = 0) -> dict:
    streams_of = jax.random.split(jax.random.key(seed), 6)
    return {
        "images": noise(streams_of[0], (TOTAL, D), 0.03, 0.19921875, ((0, 128),)),
        "texts": noise(streams_of[1], (TOTAL, D), 0.03, 0.19921875, ((0, 128),)),
        "pair_ids": with_ends(jax.random.randint(streams_of[2], (TOTAL,), 0, GROUPS), jax.random.fold_in(streams_of[2], 1), 0, GROUPS - 1).astype(jnp.int32),
        "log_scale": jnp.clip(jax.random.uniform(streams_of[3], (1,), jnp.float32, 1.0, 2.3), 1.0, 2.3),
        "bias": jnp.clip(jax.random.uniform(streams_of[4], (1,), jnp.float32, -6.0, -2.0), -6.0, -2.0),
    }


def unit(rows):
    rows32 = rows.astype(jnp.float32)
    norms = jnp.sqrt(lax.optimization_barrier(jnp.sum(rows32 * rows32, axis=1, keepdims=True)) + 1e-06)
    return (rows32 / norms, norms)

def weights(image_block, text_block, image_labels, text_labels, log_scale, bias):
    scale = jnp.exp(log_scale[0])
    logits = scale * lax.dot_general(image_block, text_block, (((1,), (1,)), ((), ())), preferred_element_type=jnp.float32) + bias[0]
    signs = jnp.where(image_labels[:, None] == text_labels[None, :], 1.0, -1.0).astype(jnp.float32)
    return (scale * -signs * jax.nn.sigmoid(-signs * logits)).astype(jnp.bfloat16)

def back_through(exact, norms, grad):
    return (grad - exact * lax.optimization_barrier(jnp.sum(exact * grad, axis=1, keepdims=True))) / norms

def reference(images, texts, pair_ids, log_scale, bias):
    image_exact, image_norms = unit(images)
    image_unit = image_exact.astype(jnp.bfloat16)
    text_exact, text_norms = unit(texts)
    text_unit = text_exact.astype(jnp.bfloat16)
    span = STEPS * ROWS
    text_ext = jnp.concatenate([text_unit, text_unit[:span]], axis=0)
    ids_ext = jnp.concatenate([pair_ids, pair_ids[:span]], axis=0)
    blocks = TOTAL // ROWS

    def one_block(accum, index):
        start = (index * ROWS).astype(jnp.int32)
        image_block = lax.dynamic_slice_in_dim(image_unit, start, ROWS, 0)
        image_labels = lax.dynamic_slice_in_dim(pair_ids, start, ROWS, 0)
        window = lax.dynamic_slice_in_dim(text_ext, start, span, 0)
        window_labels = lax.dynamic_slice_in_dim(ids_ext, start, span, 0)
        coef = weights(image_block, window, image_labels, window_labels, log_scale, bias)
        grad_image = jnp.dot(coef, window, preferred_element_type=jnp.float32)
        grad_window = lax.dot_general(coef, image_block, (((0,), (0,)), ((), ())), preferred_element_type=jnp.float32)
        before = lax.dynamic_slice_in_dim(accum, start, span, 0)
        accum = lax.dynamic_update_slice_in_dim(accum, before + grad_window, start, 0)
        return (accum, grad_image)
    accum = jnp.zeros((TOTAL + span, D), jnp.float32)
    accum, grad_blocks = lax.scan(one_block, accum, jnp.arange(blocks, dtype=jnp.int32))
    grad_image_unit = grad_blocks.reshape(TOTAL, D)
    grad_text_unit = accum[:TOTAL].at[:span].add(accum[TOTAL:])
    return (back_through(image_exact, image_norms, grad_image_unit), back_through(text_exact, text_norms, grad_text_unit))
```

```python
import functools

import jax
import jax.numpy as jnp
from jax import lax
from jax.experimental import pallas as pl
from jax.experimental.pallas import tpu as pltpu
from jax.sharding import PartitionSpec as P

AXIS = "dp"
TILE = 256
PIECES = (384, 256, 128)
LIMIT = 24 * 1024 * 1024
HBM = pl.BlockSpec(memory_space=pl.ANY)
SMEM = pl.BlockSpec(memory_space=pltpu.SMEM)


def is_even():
    return lax.rem(lax.axis_index(AXIS), 2) == 0


def call(kernel, **kw):
    return pl.pallas_call(
        kernel, compiler_params=pltpu.CompilerParams(vmem_limit_bytes=LIMIT), **kw
    )


def inverse_norm(rows32):
    return 1.0 / jnp.sqrt(jnp.sum(rows32 * rows32, axis=1, keepdims=True) + 1e-06)


def unit(raw):
    rows32 = raw.astype(jnp.float32)
    return (rows32 * inverse_norm(rows32)).astype(jnp.bfloat16)


def pick_kernel(images, texts, out, sems):
    rows = out.shape[0]
    part = rows // sems.shape[0]

    def copy_from(src):
        copies = [
            pltpu.make_async_copy(
                src.at[pl.ds(i * part, part)], out.at[pl.ds(i * part, part)], sems.at[i]
            )
            for i in range(sems.shape[0])
        ]
        for copy in copies:
            copy.start()
        for copy in copies:
            copy.wait()

    @pl.when(is_even())
    def _():
        copy_from(texts)

    @pl.when(jnp.logical_not(is_even()))
    def _():
        copy_from(images)


def pick(images, texts):
    return call(
        pick_kernel,
        out_shape=jax.ShapeDtypeStruct(images.shape, images.dtype),
        in_specs=[HBM, HBM],
        out_specs=HBM,
        scratch_shapes=[pltpu.SemaphoreType.DMA((4,))],
        name="pick",
    )(images, texts)


def own_units_kernel(images, texts, u_raw, u_unit, v_unit):
    image_unit, text_unit = unit(images[...]), unit(texts[...])

    @pl.when(is_even())
    def _():
        u_raw[...] = images[...]
        u_unit[...] = image_unit
        v_unit[...] = text_unit

    @pl.when(jnp.logical_not(is_even()))
    def _():
        u_raw[...] = texts[...]
        u_unit[...] = text_unit
        v_unit[...] = image_unit


def own_units(images, texts):
    rows, width = images.shape
    tile = pl.BlockSpec((TILE, width), lambda i: (i, 0))
    shape = jax.ShapeDtypeStruct(images.shape, images.dtype)
    return call(
        own_units_kernel,
        grid=(rows // TILE,),
        out_shape=[shape] * 3,
        in_specs=[tile] * 2,
        out_specs=[tile] * 3,
        name="own_units",
    )(images, texts)


def units_kernel(raw, out):
    out[...] = unit(raw[...])


def units(raw):
    rows, width = raw.shape
    tile = pl.BlockSpec((TILE, width), lambda i: (i, 0))
    return call(
        units_kernel,
        grid=(rows // TILE,),
        out_shape=jax.ShapeDtypeStruct(raw.shape, raw.dtype),
        in_specs=[tile],
        out_specs=tile,
        name="units",
    )(raw)


def contribution(log_scale, bias, labels_x, labels_y, x, y):
    logits = lax.dot_general(x, y, (((1,), (1,)), ((), ())), preferred_element_type=jnp.float32)
    scale = jnp.exp(jnp.full((1, y.shape[0]), log_scale[0], jnp.float32))
    logits = scale * logits + bias[0]
    same = labels_x == labels_y
    size = scale / (1.0 + jnp.exp(jnp.where(same, logits, -logits)))
    coef = jnp.where(same, -size, size).astype(jnp.bfloat16)
    return jnp.dot(coef, y, preferred_element_type=jnp.float32)


def score_kernel(add, copy_x, pieces, *refs):
    log_scale, bias, labels_x, labels_y, x, y = refs[:6]
    refs = refs[6:]
    if add:
        before, refs = refs[0], refs[1:]
    out, refs = refs[0], refs[1:]
    if copy_x:
        x_again, refs = refs[0], refs[1:]
        x_again[...] = x[...]
    copies = []
    start = 0
    for i, size in enumerate(pieces):
        copies.append(
            pltpu.make_async_copy(
                y.at[pl.ds(start, size)], refs[i], refs[len(pieces)].at[i]
            )
        )
        start += size
    if pieces:

        @pl.when(pl.program_id(0) == 0)
        def _():
            for copy in copies:
                copy.start()

    grad = contribution(log_scale, bias, labels_x[...], labels_y[...], x[...], y[...])
    out[...] = before[...] + grad if add else grad
    if pieces:

        @pl.when(pl.program_id(0) == pl.num_programs(0) - 1)
        def _():
            for copy in copies:
                copy.wait()


def score(scalars, labels_x, labels_y, x, y, before=None, copy_x=False, pieces=()):
    rows, width = x.shape
    tile = pl.BlockSpec((TILE, width), lambda i: (i, 0))
    column = pl.BlockSpec((TILE, 1), lambda i: (i, 0))
    whole = pl.BlockSpec(y.shape, lambda i: (0, 0))
    line = pl.BlockSpec((1, y.shape[0]), lambda i: (0, 0))
    args = [*scalars, labels_x, labels_y, x, y]
    in_specs = [SMEM, SMEM, column, line, tile, whole]
    aliases = {}
    if before is not None:
        aliases = {len(args): 0}
        args.append(before)
        in_specs.append(tile)
    out_shape = [jax.ShapeDtypeStruct(x.shape, jnp.float32)]
    out_specs = [tile]
    if copy_x:
        out_shape.append(jax.ShapeDtypeStruct(x.shape, x.dtype))
        out_specs.append(tile)
    for size in pieces:
        out_shape.append(jax.ShapeDtypeStruct((size, width), y.dtype))
        out_specs.append(HBM)
    return call(
        functools.partial(score_kernel, before is not None, copy_x, pieces),
        grid=(rows // TILE,),
        out_shape=out_shape,
        in_specs=in_specs,
        out_specs=out_specs,
        input_output_aliases=aliases,
        scratch_shapes=[pltpu.SemaphoreType.DMA((len(pieces),))] if pieces else [],
        name="score",
    )(*args)


def finish_kernel(to_images_on_even, continued, *refs):
    log_scale, bias, labels_x, labels_y, x, y, before, raw = refs[:8]
    image_grad, text_grad, stage, sems = refs[10 if continued else 8 :]
    step = pl.program_id(0)
    grad = before[...] + contribution(
        log_scale, bias, labels_x[...], labels_y[...], x[...], y[...]
    )
    rows32 = raw[...].astype(jnp.float32)
    inverse = inverse_norm(rows32)
    exact = rows32 * inverse
    stage[step] = (grad - exact * jnp.sum(exact * grad, axis=1, keepdims=True)) * inverse
    to_images = is_even() if to_images_on_even else jnp.logical_not(is_even())

    def copy(out, i):
        return pltpu.make_async_copy(stage.at[i], out.at[pl.ds(i * TILE, TILE)], sems.at[i])

    for out, here in ((image_grad, to_images), (text_grad, jnp.logical_not(to_images))):

        @pl.when(here)
        def _(out=out):
            copy(out, step).start()

            @pl.when(step == pl.num_programs(0) - 1)
            def _():
                for i in range(stage.shape[0]):
                    copy(out, i).wait()


def finish(scalars, labels_x, labels_y, x, y, before, raw, to_images_on_even, outs=None):
    rows, width = x.shape
    tile = pl.BlockSpec((TILE, width), lambda i: (i, 0))
    column = pl.BlockSpec((TILE, 1), lambda i: (i, 0))
    whole = pl.BlockSpec(y.shape, lambda i: (0, 0))
    line = pl.BlockSpec((1, y.shape[0]), lambda i: (0, 0))
    args = [*scalars, labels_x, labels_y, x, y, before, raw]
    in_specs = [SMEM, SMEM, column, line, tile, whole, tile, tile]
    aliases = {}
    if outs is not None:
        aliases = {len(args): 0, len(args) + 1: 1}
        args += list(outs)
        in_specs += [HBM, HBM]
    return call(
        functools.partial(finish_kernel, to_images_on_even, outs is not None),
        grid=(rows // TILE,),
        out_shape=[jax.ShapeDtypeStruct(x.shape, jnp.float32)] * 2,
        in_specs=in_specs,
        out_specs=[HBM, HBM],
        input_output_aliases=aliases,
        scratch_shapes=[
            pltpu.VMEM((rows // TILE, TILE, width), jnp.float32),
            pltpu.SemaphoreType.DMA((rows // TILE,)),
        ],
        name="finish",
    )(*args)


def permute(value, even_step, odd_step):
    count = lax.axis_size(AXIS)
    pairs = [(p, (p + (odd_step if p % 2 else even_step)) % count) for p in range(count)]
    return lax.ppermute(value, AXIS, pairs)


def swap(value):
    return permute(value, 1, -1)


def on_device(images, texts, pair_ids, log_scale, bias):
    rows = images.shape[0]
    count = lax.axis_size(AXIS)
    me = lax.axis_index(AXIS)
    scalars = (log_scale, bias)

    v_raw = pick(images, texts)
    x_raw = permute(v_raw, -1, 1)

    all_ids = lax.all_gather(pair_ids, AXIS)
    sign = jnp.where(me % 2 == 0, 1, -1)
    away = sign * jnp.array([0, 1, -1, 2, 3, -2, -3], jnp.int32)
    near = all_ids[(me + away + count) % count]
    own, from_s0, from_x, from_s1, from_y, from_s2, from_z = [near[i : i + 1] for i in range(7)]
    labels = pair_ids.reshape(rows, 1)
    own = pair_ids.reshape(1, rows)

    u_raw, u_unit, v_unit = own_units(images, texts)
    s0 = swap(u_unit)
    (grad_u,) = score(scalars, labels, own, u_unit, v_unit)
    (grad_v,) = score(scalars, labels, own, v_unit, u_unit)
    grad_u, u_again = score(scalars, labels, from_s0, u_unit, s0, grad_u, copy_x=True)
    y = permute(u_again, 3, -3)

    x = units(x_raw)
    s1 = swap(x)
    grad_v, *parts = score(scalars, labels, from_x, v_unit, x, grad_v, pieces=PIECES)
    z = [permute(part, 2, -2) for part in parts]
    (grad_u,) = score(scalars, labels, from_s1, u_unit, s1, grad_u)

    s2 = swap(y)
    outs = finish(scalars, labels, from_y, u_unit, y, grad_u, u_raw, True)
    (grad_v,) = score(scalars, labels, from_s2, v_unit, s2, grad_v)

    start = 0
    for size, part in zip(PIECES, z):
        here = from_z[:, start : start + size]
        start += size
        if start < rows:
            (grad_v,) = score(scalars, labels, here, v_unit, part, grad_v)
        else:
            outs = finish(scalars, labels, here, v_unit, part, grad_v, v_raw, False, outs)
    return tuple(outs)


def solution(mesh):
    in_specs = (P("dp", None), P("dp", None), P("dp"), P(), P())
    out_specs = (P("dp", None), P("dp", None))
    return jax.shard_map(
        on_device, mesh=mesh, in_specs=in_specs, out_specs=out_specs, check_vma=False
    )
```

```python
import functools

import jax
import jax.numpy as jnp
from jax import lax
from jax.experimental import pallas as pl
from jax.experimental.pallas import tpu as pltpu
from jax.sharding import PartitionSpec as P

AXIS = "dp"
TILE = 256
ROWS = 768
LABEL_ROWS = 16
PIECES = (384, 256, 128)
PARTS = 4
LIMIT = 16 * 1024 * 1024
LOG2E = 1.4426950408889634
MICROSECOND = 1.0e9
ANY = pl.BlockSpec(memory_space=pl.ANY)
HBM = pl.BlockSpec(memory_space=pltpu.HBM)
VMEM = pl.BlockSpec(memory_space=pltpu.VMEM)
SMEM = pl.BlockSpec(memory_space=pltpu.SMEM)


def is_even():
    return lax.rem(lax.axis_index(AXIS), 2) == 0


def call(kernel, args, in_specs, out_shape, cost=1, **kw):
    places = {id(VMEM): pltpu.VMEM, id(HBM): pltpu.HBM}
    args = [
        pltpu.with_memory_space_constraint(arg, places[id(spec)]) if id(spec) in places else arg
        for arg, spec in zip(args, in_specs)
    ]
    return pl.pallas_call(
        kernel,
        out_shape=out_shape,
        in_specs=in_specs,
        compiler_params=pltpu.CompilerParams(vmem_limit_bytes=LIMIT),
        cost_estimate=pl.CostEstimate(
            flops=int(cost * MICROSECOND), bytes_accessed=0, transcendentals=0
        ),
        **kw,
    )(*args)


def inverse_norm(rows32):
    return 1.0 / jnp.sqrt(jnp.sum(rows32 * rows32, axis=1, keepdims=True) + 1e-06)


def unit(raw):
    rows32 = raw.astype(jnp.float32)
    return (rows32 * inverse_norm(rows32)).astype(jnp.bfloat16)


def put_units(raw, out):
    for start in range(0, ROWS, TILE):
        rows = pl.ds(start, TILE)
        out[rows, :] = unit(raw[rows, :])
    out[ROWS:, :] = raw[ROWS:, :]


def put_labels(ids, out):
    out[ROWS:, :] = jnp.zeros((LABEL_ROWS, out.shape[1]), out.dtype)
    labels = jnp.broadcast_to(ids[...], (LABEL_ROWS, ROWS)).astype(jnp.float32)
    out[ROWS:, :ROWS] = labels.astype(out.dtype)


def pick_copies(src, out, sems):
    part = ROWS // PARTS
    return [
        pltpu.make_async_copy(
            src.at[pl.ds(i * part, part)], out.at[pl.ds(i * part, part)], sems.at[i]
        )
        for i in range(PARTS)
    ]


def start_pick(take_texts, images, texts, out, sems):
    for src, here in ((texts, take_texts), (images, jnp.logical_not(take_texts))):

        @pl.when(here)
        def _(src=src):
            for copy in pick_copies(src, out, sems):
                copy.start()


def wait_pick(images, out, sems):
    for copy in pick_copies(images, out, sems):
        copy.wait()


def first_kernel(images, texts, ids, v_raw, sems):
    start_pick(is_even(), images, texts, v_raw, sems)
    put_labels(ids, v_raw)
    wait_pick(images, v_raw, sems)


def first(images, texts, ids):
    return call(
        first_kernel,
        [images, texts, ids],
        [HBM, HBM, VMEM],
        pltpu.VMEM((ROWS + LABEL_ROWS, images.shape[1]), images.dtype),
        out_specs=VMEM,
        scratch_shapes=[pltpu.SemaphoreType.DMA((PARTS,))],
        name="first",
    )


def second_kernel(images, texts, ids, v_raw, u_raw, u, v, sems):
    start_pick(jnp.logical_not(is_even()), images, texts, u_raw, sems)
    put_labels(ids, u_raw)
    put_units(v_raw, v)
    wait_pick(images, u_raw, sems)
    put_units(u_raw, u)


def second(images, texts, ids, v_raw):
    return call(
        second_kernel,
        [images, texts, ids, v_raw],
        [HBM, HBM, VMEM, VMEM],
        [pltpu.VMEM(v_raw.shape, v_raw.dtype)] * 3,
        out_specs=[VMEM] * 3,
        scratch_shapes=[pltpu.SemaphoreType.DMA((PARTS,))],
        name="second",
        cost=2,
    )


def units(raw):
    return call(
        put_units,
        [raw],
        [VMEM],
        pltpu.VMEM(raw.shape, raw.dtype),
        out_specs=VMEM,
        name="units",
        cost=0.7,
    )


def cut_kernel(value, later, *outs):
    start = 0
    for out in outs:
        size = out.shape[0] if len(outs) == 1 or start else out.shape[0] - LABEL_ROWS
        out[:size, :] = value[pl.ds(start, size), :]
        if size < out.shape[0]:
            out[size:, :] = value[ROWS:, :]
        start += size


def cut(value, later, sizes):
    return call(
        cut_kernel,
        [value, later],
        [VMEM, ANY],
        [pltpu.VMEM((size, value.shape[1]), value.dtype) for size in sizes],
        out_specs=[VMEM] * len(sizes),
        name="cut",
        cost=0.2,
    )


def contributions(log_scale, bias, labels_x, labels_y, x, y, size):
    scale = jnp.exp(jnp.full((1, size), log_scale[0], jnp.float32))
    rate = scale * -LOG2E
    shift = bias[0] * -LOG2E
    tiles = [pl.ds(start, TILE) for start in range(0, ROWS, TILE)]

    def products(rows):
        return lax.dot_general(
            x[rows, :], y[:size, :], (((1,), (1,)), ((), ())), preferred_element_type=jnp.float32
        )

    ahead = products(tiles[0])
    for i, rows in enumerate(tiles):
        now = ahead
        if i + 1 < len(tiles):
            ahead = products(tiles[i + 1])
        sigmoid = 1.0 / (1.0 + jnp.exp2(now * rate + shift))
        same = jnp.where(labels_x[rows, :] == labels_y, 1.0, 0.0)
        coef = ((sigmoid - same) * scale).astype(jnp.bfloat16)
        yield rows, jnp.dot(coef, y[:size, :], preferred_element_type=jnp.float32)


def line_of(labelled, labels_at, start, size):
    lines = labelled[labels_at : labels_at + LABEL_ROWS, :].astype(jnp.float32)
    return lines[:1, start : start + size]


def score_kernel(where, log_scale, bias, labels_x, x, y, *refs):
    labels_at, start, size = where
    labelled = y
    if labels_at + LABEL_ROWS > y.shape[0]:
        labelled, refs = refs[0], refs[1:]
    out = refs[-1]
    labels_y = line_of(labelled, labels_at, start, size)
    for rows, grad in contributions(log_scale, bias, labels_x, labels_y, x, y, size):
        out[rows, :] = refs[0][rows, :] + grad if len(refs) > 1 else grad


def score_args(scalars, labels_x, x, y, labelled, labels_at, start):
    size = y.shape[0] if labelled is not None else labels_at
    args = [*scalars, labels_x, x, y] + ([labelled] if labelled is not None else [])
    in_specs = [SMEM, SMEM] + [VMEM] * (len(args) - 2)
    cost = 3.5 * size / ROWS
    return args, in_specs, (labels_at, start, size), cost


def score(scalars, labels_x, x, y, before=None, labelled=None, labels_at=ROWS, start=0):
    args, in_specs, where, cost = score_args(
        scalars, labels_x, x, y, labelled, labels_at, start
    )
    aliases = {}
    if before is not None:
        aliases = {len(args): 0}
        args.append(before)
        in_specs.append(VMEM)
    return call(
        functools.partial(score_kernel, where),
        args,
        in_specs,
        pltpu.VMEM((ROWS, x.shape[1]), jnp.float32),
        out_specs=VMEM,
        input_output_aliases=aliases,
        name="score",
        cost=cost,
    )


def finish_kernel(where, to_images_on_even, continued, *refs):
    labels_at, start, size = where
    log_scale, bias, labels_x, x, y = refs[:5]
    refs = refs[5:]
    labelled = y
    if labels_at + LABEL_ROWS > y.shape[0]:
        labelled, refs = refs[0], refs[1:]
    before, raw = refs[:2]
    image_grad, text_grad, stage, sems = refs[4 if continued else 2 :]
    to_images = is_even() if to_images_on_even else jnp.logical_not(is_even())
    places = ((image_grad, to_images), (text_grad, jnp.logical_not(to_images)))

    def copy(out, rows, i):
        return pltpu.make_async_copy(stage.at[rows], out.at[rows], sems.at[i])

    labels_y = line_of(labelled, labels_at, start, size)
    steps = []
    for rows, grad in contributions(log_scale, bias, labels_x, labels_y, x, y, size):
        grad = before[rows, :] + grad
        rows32 = raw[rows, :].astype(jnp.float32)
        inverse = inverse_norm(rows32)
        exact = rows32 * inverse
        stage[rows, :] = (grad - exact * jnp.sum(exact * grad, axis=1, keepdims=True)) * inverse
        for out, here in places:
            pl.when(here)(copy(out, rows, len(steps)).start)
        steps.append(rows)
    for i, rows in enumerate(steps):
        copy(image_grad, rows, i).wait()


def finish(
    scalars,
    labels_x,
    x,
    y,
    before,
    raw,
    to_images_on_even,
    outs=None,
    labelled=None,
    labels_at=ROWS,
    start=0,
):
    args, in_specs, where, cost = score_args(
        scalars, labels_x, x, y, labelled, labels_at, start
    )
    args += [before, raw]
    in_specs += [VMEM, VMEM]
    aliases = {}
    if outs is not None:
        aliases = {len(args): 0, len(args) + 1: 1}
        args += list(outs)
        in_specs += [HBM, HBM]
    shape = (ROWS, x.shape[1])
    return call(
        functools.partial(finish_kernel, where, to_images_on_even, outs is not None),
        args,
        in_specs,
        [pltpu.HBM(shape, jnp.float32)] * 2,
        out_specs=[HBM, HBM],
        input_output_aliases=aliases,
        scratch_shapes=[
            pltpu.VMEM(shape, jnp.float32),
            pltpu.SemaphoreType.DMA((ROWS // TILE,)),
        ],
        name="finish",
        cost=cost + 2,
    )


def permute(value, even_step, odd_step):
    count = lax.axis_size(AXIS)
    pairs = [(p, (p + (odd_step if p % 2 else even_step)) % count) for p in range(count)]
    return lax.ppermute(value, AXIS, pairs)


def swap(value):
    return permute(value, 1, -1)


def on_device(images, texts, pair_ids, log_scale, bias):
    scalars = (log_scale, bias)
    ids = pair_ids.reshape(1, ROWS)
    labels = pair_ids.astype(jnp.float32).reshape(ROWS, 1)

    v_raw = first(images, texts, ids)
    x_raw = permute(v_raw, -1, 1)
    u_raw, u, v = second(images, texts, ids, v_raw)
    s0 = swap(u)
    grad_u = score(scalars, labels, u, v)
    grad_v = score(scalars, labels, v, u)
    (u_again,) = cut(u, grad_v, (u.shape[0],))
    y = permute(u_again, 3, -3)
    grad_u = score(scalars, labels, u, s0, grad_u)

    x = units(x_raw)
    s1 = swap(x)
    grad_v = score(scalars, labels, v, x, grad_v)
    grad_u = score(scalars, labels, u, s1, grad_u)
    sizes = (PIECES[0] + LABEL_ROWS, *PIECES[1:])
    z = [permute(piece, 2, -2) for piece in cut(x, grad_u, sizes)]

    s2 = swap(y)
    outs = finish(scalars, labels, u, y, grad_u, u_raw, True)
    grad_v = score(scalars, labels, v, s2, grad_v)

    grad_v = score(scalars, labels, v, z[0], grad_v, labels_at=PIECES[0])
    start = PIECES[0]
    for piece in z[1:]:
        place = dict(labelled=z[0], labels_at=PIECES[0], start=start)
        start += piece.shape[0]
        if start < ROWS:
            grad_v = score(scalars, labels, v, piece, grad_v, **place)
        else:
            outs = finish(scalars, labels, v, piece, grad_v, v_raw, False, outs, **place)
    return tuple(outs)


def solution(mesh):
    in_specs = (P("dp", None), P("dp", None), P("dp"), P(), P())
    out_specs = (P("dp", None), P("dp", None))
    return jax.shard_map(
        on_device, mesh=mesh, in_specs=in_specs, out_specs=out_specs, check_vma=False
    )
```

```python
import functools

import jax
import jax.numpy as jnp
from jax import lax
from jax.experimental import pallas as pl
from jax.experimental.pallas import tpu as pltpu
from jax.sharding import PartitionSpec as P

AXIS = "dp"
TILE = 256
ROWS = 768
LABEL_ROWS = 16
PIECES = (384, 256, 128)
PARTS = 4
LIMIT = 16 * 1024 * 1024
LOG2E = 1.4426950408889634
ANY = pl.BlockSpec(memory_space=pl.ANY)
HBM = pl.BlockSpec(memory_space=pltpu.HBM)
VMEM = pl.BlockSpec(memory_space=pltpu.VMEM)
SMEM = pl.BlockSpec(memory_space=pltpu.SMEM)


def is_even():
    return lax.rem(lax.axis_index(AXIS), 2) == 0


class Order:
    def __init__(self):
        self.token = None

    def __call__(self, kernel, args, in_specs, out_shape, out_specs, scratch_shapes=(), **kw):
        places = {id(VMEM): pltpu.VMEM, id(HBM): pltpu.HBM}
        single = not isinstance(out_shape, list)
        out_shape = [out_shape] if single else out_shape
        out_specs = [out_specs] if single else out_specs
        args = [
            pltpu.with_memory_space_constraint(arg, places[id(spec)]) if id(spec) in places else arg
            for arg, spec in zip(args, in_specs)
        ]
        n_in, n_out, first = len(args), len(out_shape), self.token is None
        if not first:
            args = [*args, self.token]
            in_specs = [*in_specs, ANY]

        def without_tokens(*refs):
            rest = refs[len(args) :]
            kernel(*refs[:n_in], *rest[:n_out], *rest[n_out + 1 :])

        *outs, self.token = pl.pallas_call(
            without_tokens,
            out_shape=[*out_shape, pltpu.VMEM((8, 128), jnp.float32)],
            in_specs=in_specs,
            out_specs=[*out_specs, VMEM],
            scratch_shapes=scratch_shapes,
            compiler_params=pltpu.CompilerParams(vmem_limit_bytes=LIMIT),
            cost_estimate=pl.CostEstimate(flops=int(20e9), bytes_accessed=0, transcendentals=0),
            **kw,
        )(*args)
        return outs[0] if single else outs


def inverse_norm(rows32):
    return 1.0 / jnp.sqrt(jnp.sum(rows32 * rows32, axis=1, keepdims=True) + 1e-06)


def unit(raw):
    rows32 = raw.astype(jnp.float32)
    return (rows32 * inverse_norm(rows32)).astype(jnp.bfloat16)


def put_units(raw, out):
    for start in range(0, ROWS, TILE):
        rows = pl.ds(start, TILE)
        out[rows, :] = unit(raw[rows, :])
    out[ROWS:, :] = raw[ROWS:, :]


def put_labels(ids, out):
    out[ROWS:, :] = jnp.zeros((LABEL_ROWS, out.shape[1]), out.dtype)
    labels = jnp.broadcast_to(ids[...], (LABEL_ROWS, ROWS)).astype(jnp.float32)
    out[ROWS:, :ROWS] = labels.astype(out.dtype)


def pick_copies(src, out, sems):
    part = ROWS // PARTS
    return [
        pltpu.make_async_copy(
            src.at[pl.ds(i * part, part)], out.at[pl.ds(i * part, part)], sems.at[i]
        )
        for i in range(PARTS)
    ]


def start_pick(take_texts, images, texts, out, sems):
    for src, here in ((texts, take_texts), (images, jnp.logical_not(take_texts))):

        @pl.when(here)
        def _(src=src):
            for copy in pick_copies(src, out, sems):
                copy.start()


def wait_pick(images, out, sems):
    for copy in pick_copies(images, out, sems):
        copy.wait()


def first_kernel(images, texts, ids, v_raw, sems):
    start_pick(is_even(), images, texts, v_raw, sems)
    put_labels(ids, v_raw)
    wait_pick(images, v_raw, sems)


def first(call, images, texts, ids):
    return call(
        first_kernel,
        [images, texts, ids],
        [HBM, HBM, VMEM],
        pltpu.VMEM((ROWS + LABEL_ROWS, images.shape[1]), images.dtype),
        out_specs=VMEM,
        scratch_shapes=[pltpu.SemaphoreType.DMA((PARTS,))],
        name="first",
    )


def second_kernel(images, texts, ids, v_raw, u_raw, u, v, sems):
    start_pick(jnp.logical_not(is_even()), images, texts, u_raw, sems)
    put_labels(ids, u_raw)
    put_units(v_raw, v)
    wait_pick(images, u_raw, sems)
    put_units(u_raw, u)


def second(call, images, texts, ids, v_raw):
    return call(
        second_kernel,
        [images, texts, ids, v_raw],
        [HBM, HBM, VMEM, VMEM],
        [pltpu.VMEM(v_raw.shape, v_raw.dtype)] * 3,
        out_specs=[VMEM] * 3,
        scratch_shapes=[pltpu.SemaphoreType.DMA((PARTS,))],
        name="second",
    )


def units(call, raw):
    return call(
        put_units,
        [raw],
        [VMEM],
        pltpu.VMEM(raw.shape, raw.dtype),
        out_specs=VMEM,
        name="units",
    )


def cut_kernel(value, *outs):
    start = 0
    for out in outs:
        size = out.shape[0] if len(outs) == 1 or start else out.shape[0] - LABEL_ROWS
        out[:size, :] = value[pl.ds(start, size), :]
        if size < out.shape[0]:
            out[size:, :] = value[ROWS:, :]
        start += size


def cut(call, value, sizes):
    return call(
        cut_kernel,
        [value],
        [VMEM],
        [pltpu.VMEM((size, value.shape[1]), value.dtype) for size in sizes],
        out_specs=[VMEM] * len(sizes),
        name="cut",
    )


def contributions(log_scale, bias, labels_x, labels_y, x, y, size):
    scale = jnp.exp(jnp.full((1, size), log_scale[0], jnp.float32))
    rate = scale * -LOG2E
    shift = bias[0] * -LOG2E
    tiles = [pl.ds(start, TILE) for start in range(0, ROWS, TILE)]

    def products(rows):
        return lax.dot_general(
            x[rows, :], y[:size, :], (((1,), (1,)), ((), ())), preferred_element_type=jnp.float32
        )

    ahead = products(tiles[0])
    for i, rows in enumerate(tiles):
        now = ahead
        if i + 1 < len(tiles):
            ahead = products(tiles[i + 1])
        sigmoid = 1.0 / (1.0 + jnp.exp2(now * rate + shift))
        same = jnp.where(labels_x[rows, :] == labels_y, 1.0, 0.0)
        coef = ((sigmoid - same) * scale).astype(jnp.bfloat16)
        yield rows, jnp.dot(coef, y[:size, :], preferred_element_type=jnp.float32)


def line_of(labelled, labels_at, start, size):
    lines = labelled[labels_at : labels_at + LABEL_ROWS, :].astype(jnp.float32)
    return lines[:1, start : start + size]


def score_kernel(where, log_scale, bias, labels_x, x, y, *refs):
    labels_at, start, size = where
    labelled = y
    if labels_at + LABEL_ROWS > y.shape[0]:
        labelled, refs = refs[0], refs[1:]
    out = refs[-1]
    labels_y = line_of(labelled, labels_at, start, size)
    for rows, grad in contributions(log_scale, bias, labels_x, labels_y, x, y, size):
        out[rows, :] = refs[0][rows, :] + grad if len(refs) > 1 else grad


def score_args(scalars, labels_x, x, y, labelled, labels_at, start):
    size = y.shape[0] if labelled is not None else labels_at
    args = [*scalars, labels_x, x, y] + ([labelled] if labelled is not None else [])
    in_specs = [SMEM, SMEM] + [VMEM] * (len(args) - 2)
    return args, in_specs, (labels_at, start, size)


def score(call, scalars, labels_x, x, y, before=None, labelled=None, labels_at=ROWS, start=0):
    args, in_specs, where = score_args(
        scalars, labels_x, x, y, labelled, labels_at, start
    )
    aliases = {}
    if before is not None:
        aliases = {len(args): 0}
        args.append(before)
        in_specs.append(VMEM)
    return call(
        functools.partial(score_kernel, where),
        args,
        in_specs,
        pltpu.VMEM((ROWS, x.shape[1]), jnp.float32),
        out_specs=VMEM,
        input_output_aliases=aliases,
        name="score",
    )


def finish_kernel(where, to_images_on_even, continued, *refs):
    labels_at, start, size = where
    log_scale, bias, labels_x, x, y = refs[:5]
    refs = refs[5:]
    labelled = y
    if labels_at + LABEL_ROWS > y.shape[0]:
        labelled, refs = refs[0], refs[1:]
    before, raw = refs[:2]
    image_grad, text_grad, stage, sems = refs[4 if continued else 2 :]
    to_images = is_even() if to_images_on_even else jnp.logical_not(is_even())
    places = ((image_grad, to_images), (text_grad, jnp.logical_not(to_images)))

    def copy(out, rows, i):
        return pltpu.make_async_copy(stage.at[rows], out.at[rows], sems.at[i])

    labels_y = line_of(labelled, labels_at, start, size)
    steps = []
    for rows, grad in contributions(log_scale, bias, labels_x, labels_y, x, y, size):
        grad = before[rows, :] + grad
        rows32 = raw[rows, :].astype(jnp.float32)
        inverse = inverse_norm(rows32)
        exact = rows32 * inverse
        stage[rows, :] = (grad - exact * jnp.sum(exact * grad, axis=1, keepdims=True)) * inverse
        for out, here in places:
            pl.when(here)(copy(out, rows, len(steps)).start)
        steps.append(rows)
    for i, rows in enumerate(steps):
        copy(image_grad, rows, i).wait()


def finish(
    call,
    scalars,
    labels_x,
    x,
    y,
    before,
    raw,
    to_images_on_even,
    outs=None,
    labelled=None,
    labels_at=ROWS,
    start=0,
):
    args, in_specs, where = score_args(
        scalars, labels_x, x, y, labelled, labels_at, start
    )
    args += [before, raw]
    in_specs += [VMEM, VMEM]
    aliases = {}
    if outs is not None:
        aliases = {len(args): 0, len(args) + 1: 1}
        args += list(outs)
        in_specs += [HBM, HBM]
    shape = (ROWS, x.shape[1])
    return call(
        functools.partial(finish_kernel, where, to_images_on_even, outs is not None),
        args,
        in_specs,
        [pltpu.HBM(shape, jnp.float32)] * 2,
        out_specs=[HBM, HBM],
        input_output_aliases=aliases,
        scratch_shapes=[
            pltpu.VMEM(shape, jnp.float32),
            pltpu.SemaphoreType.DMA((ROWS // TILE,)),
        ],
        name="finish",
    )


def permute(value, even_step, odd_step):
    count = lax.axis_size(AXIS)
    pairs = [(p, (p + (odd_step if p % 2 else even_step)) % count) for p in range(count)]
    return lax.ppermute(value, AXIS, pairs)


def swap(value):
    return permute(value, 1, -1)


def on_device(images, texts, pair_ids, log_scale, bias):
    call = Order()
    scalars = (log_scale, bias)
    ids = pair_ids.reshape(1, ROWS)
    labels = pair_ids.astype(jnp.float32).reshape(ROWS, 1)

    v_raw = first(call, images, texts, ids)
    x_raw = permute(v_raw, -1, 1)
    u_raw, u, v = second(call, images, texts, ids, v_raw)
    s0 = swap(u)
    grad_u = score(call, scalars, labels, u, v)
    grad_v = score(call, scalars, labels, v, u)
    (u_again,) = cut(call, u, (u.shape[0],))
    y = permute(u_again, 3, -3)
    grad_u = score(call, scalars, labels, u, s0, grad_u)

    x = units(call, x_raw)
    s1 = swap(x)
    grad_v = score(call, scalars, labels, v, x, grad_v)
    sizes = (PIECES[0] + LABEL_ROWS, *PIECES[1:])
    z = [permute(piece, 2, -2) for piece in cut(call, x, sizes)]
    grad_u = score(call, scalars, labels, u, s1, grad_u)

    (y_again,) = cut(call, y, (y.shape[0],))
    s2 = swap(y_again)
    outs = finish(call, scalars, labels, u, y, grad_u, u_raw, True)
    grad_v = score(call, scalars, labels, v, s2, grad_v)

    grad_v = score(call, scalars, labels, v, z[0], grad_v, labels_at=PIECES[0])
    start = PIECES[0]
    for piece in z[1:]:
        place = dict(labelled=z[0], labels_at=PIECES[0], start=start)
        start += piece.shape[0]
        if start < ROWS:
            grad_v = score(call, scalars, labels, v, piece, grad_v, **place)
        else:
            outs = finish(call, scalars, labels, v, piece, grad_v, v_raw, False, outs, **place)
    return tuple(outs)


def solution(mesh):
    in_specs = (P("dp", None), P("dp", None), P("dp"), P(), P())
    out_specs = (P("dp", None), P("dp", None))
    return jax.shard_map(
        on_device, mesh=mesh, in_specs=in_specs, out_specs=out_specs, check_vma=False
    )
```

```python
import functools

import jax
import jax.numpy as jnp
from jax import lax
from jax.experimental import pallas as pl
from jax.experimental.pallas import tpu as pltpu
from jax.sharding import PartitionSpec as P

AXIS = "dp"
TILE = 256
ROWS = 768
LABEL_ROWS = 16
PIECES = (352, 416)
PARTS = 4
ADD_TILE = 32
LIMIT = 16 * 1024 * 1024
W_FINISH = 20e9
W_CLOSE = 20e9
W_COPIED = 20e9
W_ADD = 20e9
LOG2E = 1.4426950408889634
ANY = pl.BlockSpec(memory_space=pl.ANY)
HBM = pl.BlockSpec(memory_space=pltpu.HBM)
VMEM = pl.BlockSpec(memory_space=pltpu.VMEM)
SMEM = pl.BlockSpec(memory_space=pltpu.SMEM)


def is_even():
    return lax.rem(lax.axis_index(AXIS), 2) == 0


class Order:
    def __init__(self):
        self.token = None

    def __call__(
        self, kernel, args, in_specs, out_shape, out_specs, scratch_shapes=(), weight=20e9, **kw
    ):
        places = {id(VMEM): pltpu.VMEM, id(HBM): pltpu.HBM}
        single = not isinstance(out_shape, list)
        out_shape = [out_shape] if single else out_shape
        out_specs = [out_specs] if single else out_specs
        args = [
            pltpu.with_memory_space_constraint(arg, places[id(spec)]) if id(spec) in places else arg
            for arg, spec in zip(args, in_specs)
        ]
        n_in, n_out, first = len(args), len(out_shape), self.token is None
        if not first:
            args = [*args, self.token]
            in_specs = [*in_specs, ANY]

        def without_tokens(*refs):
            rest = refs[len(args) :]
            kernel(*refs[:n_in], *rest[:n_out], *rest[n_out + 1 :])

        *outs, self.token = pl.pallas_call(
            without_tokens,
            out_shape=[*out_shape, pltpu.VMEM((8, 128), jnp.float32)],
            in_specs=in_specs,
            out_specs=[*out_specs, VMEM],
            scratch_shapes=scratch_shapes,
            compiler_params=pltpu.CompilerParams(vmem_limit_bytes=LIMIT),
            cost_estimate=pl.CostEstimate(flops=int(weight), bytes_accessed=0, transcendentals=0),
            **kw,
        )(*args)
        return outs[0] if single else outs


def inverse_norm(rows32):
    return 1.0 / jnp.sqrt(jnp.sum(rows32 * rows32, axis=1, keepdims=True) + 1e-06)


def unit(raw):
    rows32 = raw.astype(jnp.float32)
    return (rows32 * inverse_norm(rows32)).astype(jnp.bfloat16)


def tiles_of(size):
    return [pl.ds(start, min(TILE, size - start)) for start in range(0, size, TILE)]


def put_units(raw, out):
    for rows in tiles_of(ROWS):
        out[rows, :] = unit(raw[rows, :])


def put_labels(ids, out):
    out[ROWS:, :] = jnp.zeros((LABEL_ROWS, out.shape[1]), out.dtype)
    labels = jnp.broadcast_to(ids, (LABEL_ROWS, ROWS)).astype(jnp.float32)
    out[ROWS:, :ROWS] = labels.astype(out.dtype)


def line_of(block):
    return block[ROWS:, :].astype(jnp.float32)[:1, :ROWS]


def either(first_here, one, other):
    pl.when(first_here)(one)
    pl.when(jnp.logical_not(first_here))(other)


def part_copies(src, out, sems):
    part = ROWS // PARTS
    return [
        pltpu.make_async_copy(
            src.at[pl.ds(i * part, part)], out.at[pl.ds(i * part, part)], sems.at[i]
        )
        for i in range(PARTS)
    ]


def column_of(ids):
    lines = jnp.broadcast_to(ids, (8, ROWS)).astype(jnp.float32)
    return jnp.transpose(lines)[:, :1]


def own_kernel(
    images, texts, pair_ids, u_raw, v_raw, u, v, ids, labels, flat, flat_sem, u_sems, v_sems
):
    ids_copy = pltpu.make_async_copy(pair_ids, flat, flat_sem)
    ids_copy.start()

    def start(first, second):
        for copy in part_copies(first, u_raw, u_sems) + part_copies(second, v_raw, v_sems):
            copy.start()

    either(is_even(), lambda: start(images, texts), lambda: start(texts, images))
    ids_copy.wait()
    ids[...] = jnp.reshape(flat[...], ids.shape)
    labels[...] = column_of(ids[...])
    put_labels(ids[...], u)
    put_labels(ids[...], v)
    for copy in part_copies(images, u_raw, u_sems):
        copy.wait()
    put_units(u_raw, u)
    for copy in part_copies(texts, v_raw, v_sems):
        copy.wait()
    put_units(v_raw, v)


def own_blocks(call, images, texts, pair_ids):
    raw = pltpu.VMEM(images.shape, images.dtype)
    labelled = pltpu.VMEM((ROWS + LABEL_ROWS, images.shape[1]), images.dtype)
    return call(
        own_kernel,
        [images, texts, pair_ids],
        [HBM] * 3,
        [
            raw,
            raw,
            labelled,
            labelled,
            pltpu.VMEM((1, ROWS), pair_ids.dtype),
            pltpu.VMEM((ROWS, 1), jnp.float32),
        ],
        out_specs=[VMEM] * 6,
        scratch_shapes=[
            pltpu.VMEM(pair_ids.shape, pair_ids.dtype),
            pltpu.SemaphoreType.DMA,
            pltpu.SemaphoreType.DMA((PARTS,)),
            pltpu.SemaphoreType.DMA((PARTS,)),
        ],
        name="own_blocks",
    )


def neighbour_kernel(left_images, right_texts, ids, raw, out, labels):
    def take(src):
        for rows in tiles_of(ROWS):
            raw[rows, :] = src[rows, :]

    either(is_even(), lambda: take(left_images), lambda: take(right_texts))
    put_units(raw, out)
    put_labels(ids[...], out)
    labels[...] = column_of(ids[...])


def neighbour_block(call, left_images, right_texts, ids):
    width = left_images.shape[1]
    return call(
        neighbour_kernel,
        [left_images, right_texts, ids],
        [VMEM] * 3,
        [
            pltpu.VMEM((ROWS, width), left_images.dtype),
            pltpu.VMEM((ROWS + LABEL_ROWS, width), left_images.dtype),
            pltpu.VMEM((ROWS, 1), jnp.float32),
        ],
        out_specs=[VMEM] * 3,
        name="neighbour_block",
    )


def copy_kernel(*refs):
    half = len(refs) // 2
    for value, out in zip(refs[:half], refs[half:]):
        out[...] = value[...]


def copied(call, *values):
    return call(
        copy_kernel,
        values,
        [VMEM] * len(values),
        [pltpu.VMEM(value.shape, value.dtype) for value in values],
        out_specs=[VMEM] * len(values),
        name="copied",
        weight=W_COPIED,
    )


def contributions(log_scale, bias, labels_x, x, y, begin=0, end=ROWS):
    scale = jnp.exp(jnp.full((1, ROWS), log_scale[0], jnp.float32))
    rate = scale * -LOG2E
    shift = bias[0] * -LOG2E
    labels_y = line_of(y)
    tiles = [
        pl.ds(start, min(TILE, end - start)) for start in range(begin, end, TILE)
    ]

    def products(rows):
        return lax.dot_general(
            x[rows, :], y[:ROWS, :], (((1,), (1,)), ((), ())), preferred_element_type=jnp.float32
        )

    ahead = products(tiles[0])
    for i, rows in enumerate(tiles):
        now = ahead
        if i + 1 < len(tiles):
            ahead = products(tiles[i + 1])
        sigmoid = 1.0 / (1.0 + jnp.exp2(now * rate + shift))
        same = jnp.where(labels_x[rows, :] == labels_y, 1.0, 0.0)
        coef = ((sigmoid - same) * scale).astype(jnp.bfloat16)
        yield rows, jnp.dot(coef, y[:ROWS, :], preferred_element_type=jnp.float32)


def back_through(raw, grad):
    rows32 = raw.astype(jnp.float32)
    inverse = inverse_norm(rows32)
    exact = rows32 * inverse
    return (grad - exact * jnp.sum(exact * grad, axis=1, keepdims=True)) * inverse


def score_kernel(log_scale, bias, labels_x, x, y, *refs):
    out = refs[-1]
    for rows, grad in contributions(log_scale, bias, labels_x, x, y):
        out[rows, :] = refs[0][rows, :] + grad if len(refs) > 1 else grad


def score(call, scalars, labels_x, x, y, before=None):
    args = [*scalars, labels_x, x, y] + ([before] if before is not None else [])
    return call(
        score_kernel,
        args,
        [SMEM, SMEM] + [VMEM] * (len(args) - 2),
        pltpu.VMEM((ROWS, x.shape[1]), jnp.float32),
        out_specs=VMEM,
        input_output_aliases={5: 0} if before is not None else {},
        name="score",
    )


def close_kernel(log_scale, bias, labels_x, x, y, before, raw, out):
    for rows, grad in contributions(log_scale, bias, labels_x, x, y):
        out[rows, :] = back_through(raw[rows, :], before[rows, :] + grad)


def close(call, scalars, labels_x, x, y, before, raw):
    args = [*scalars, labels_x, x, y, before, raw]
    return call(
        close_kernel,
        args,
        [SMEM, SMEM] + [VMEM] * (len(args) - 2),
        pltpu.VMEM((ROWS, x.shape[1]), jnp.float32),
        out_specs=VMEM,
        input_output_aliases={5: 0},
        name="close",
        weight=W_CLOSE,
    )


def part_kernel(begin, log_scale, bias, labels_x, x, y, raw, *outs):
    end = begin + sum(out.shape[0] for out in outs)
    starts = [begin + sum(out.shape[0] for out in outs[:i]) for i in range(len(outs))]
    for rows, grad in contributions(log_scale, bias, labels_x, x, y, begin, end):
        result = back_through(raw[rows, :], grad).astype(outs[0].dtype)
        for out, start in zip(outs, starts):
            low, high = max(rows.start, start), min(rows.start + rows.size, start + out.shape[0])
            if low < high:
                out[low - start : high - start, :] = result[low - rows.start : high - rows.start]


def part(call, scalars, labels_x, x, y, raw, begin, sizes):
    return call(
        functools.partial(part_kernel, begin),
        [*scalars, labels_x, x, y, raw],
        [SMEM, SMEM, VMEM, VMEM, VMEM, VMEM],
        [pltpu.VMEM((size, x.shape[1]), x.dtype) for size in sizes],
        out_specs=[VMEM] * len(sizes),
        name="part",
    )


def finish_kernel(
    log_scale, bias, labels_x, x, y, before, raw, closed, image_grad, text_grad, sems
):
    def work(target):
        copies = []
        for rows, grad in contributions(log_scale, bias, labels_x, x, y):
            closed[rows, :] = back_through(raw[rows, :], before[rows, :] + grad)
            copies.append(
                pltpu.make_async_copy(closed.at[rows], target.at[rows], sems.at[len(copies)])
            )
            copies[-1].start()
        for copy in copies:
            copy.wait()

    either(is_even(), lambda: work(image_grad), lambda: work(text_grad))


def finish(call, scalars, labels_x, x, y, before, raw):
    shape = (ROWS, x.shape[1])
    _, *outs = call(
        finish_kernel,
        [*scalars, labels_x, x, y, before, raw],
        [SMEM, SMEM] + [VMEM] * 5,
        [pltpu.VMEM(shape, jnp.float32)] + [pltpu.HBM(shape, jnp.float32)] * 2,
        out_specs=[VMEM, HBM, HBM],
        input_output_aliases={5: 0},
        scratch_shapes=[pltpu.SemaphoreType.DMA((len(tiles_of(ROWS)),))],
        name="finish",
        weight=W_FINISH,
    )
    return outs


def add_kernel(begin, _image_grad, _text_grad, closed, piece, image_grad, text_grad, stage, sems):
    tiles = [pl.ds(start, ADD_TILE) for start in range(0, piece.shape[0], ADD_TILE)]

    def work(target):
        copies = []
        for rows in tiles:
            there = pl.ds(begin + rows.start, rows.size)
            stage[rows, :] = closed[there, :] + piece[rows, :].astype(jnp.float32)
            copies.append(
                pltpu.make_async_copy(stage.at[rows], target.at[there], sems.at[len(copies)])
            )
            copies[-1].start()
        for copy in copies:
            copy.wait()

    either(is_even(), lambda: work(text_grad), lambda: work(image_grad))


def add(call, closed, piece, outs, begin):
    size, width = piece.shape
    return call(
        functools.partial(add_kernel, begin),
        [*outs, closed, piece],
        [HBM, HBM, VMEM, VMEM],
        [pltpu.HBM((ROWS, width), jnp.float32)] * 2,
        out_specs=[HBM, HBM],
        input_output_aliases={0: 0, 1: 1},
        scratch_shapes=[
            pltpu.VMEM((size, width), jnp.float32),
            pltpu.SemaphoreType.DMA((size // ADD_TILE,)),
        ],
        name="add",
        weight=W_ADD,
    )


def pairs_of(even_step, odd_step):
    count = lax.axis_size(AXIS)
    return [(p, (p + (odd_step if p % 2 else even_step)) % count) for p in range(count)]


def permute(value, even_step, odd_step):
    return lax.ppermute(value, AXIS, pairs_of(even_step, odd_step))


def swap(value):
    return permute(value, 1, -1)


def across(value):
    return permute(value, -1, 1)


def on_device(images, texts, pair_ids, log_scale, bias):
    call = Order()
    scalars = (log_scale, bias)
    left_images = permute(images, 1, 1)
    right_texts = permute(texts, -1, -1)

    u_raw, v_raw, u, v, ids, labels = own_blocks(call, images, texts, pair_ids)
    grad_u = score(call, scalars, labels, u, v)
    grad_v = score(call, scalars, labels, v, u)
    u_again, ids_again = copied(call, u, ids)
    y = permute(u_again, 3, -3)
    s0 = swap(u_again)
    near_ids = across(ids_again)

    x_raw, x, near_labels = neighbour_block(call, left_images, right_texts, near_ids)
    s1 = swap(x)
    grad_u = score(call, scalars, labels, u, s0, grad_u)
    early, late = part(call, scalars, near_labels, x, s1, x_raw, 0, PIECES)
    early, late = across(early), across(late)
    grad_v = score(call, scalars, labels, v, x, grad_v)
    grad_u = score(call, scalars, labels, u, s1, grad_u)

    s2 = swap(*copied(call, y))
    outs = finish(call, scalars, labels, u, y, grad_u, u_raw)
    closed = close(call, scalars, labels, v, s2, grad_v, v_raw)
    outs = add(call, closed, early, outs, 0)
    return tuple(add(call, closed, late, outs, PIECES[0]))


def solution(mesh):
    in_specs = (P("dp", None), P("dp", None), P("dp"), P(), P())
    out_specs = (P("dp", None), P("dp", None))
    return jax.shard_map(
        on_device, mesh=mesh, in_specs=in_specs, out_specs=out_specs, check_vma=False
    )
```

```python
import functools

import jax
import jax.numpy as jnp
from jax import lax
from jax.experimental import pallas as pl
from jax.experimental.pallas import tpu as pltpu
from jax.sharding import PartitionSpec as P

AXIS = "dp"
TILE = 256
ROWS = 768
LABEL_ROWS = 16
PIECES = (352, 416)
PARTS = 4
ADD_TILE = 32
LIMIT = 16 * 1024 * 1024
W_FINISH = 20e9
W_CLOSE = 20e9
W_COPIED = 20e9
W_ADD = 20e9
LOG2E = 1.4426950408889634
ANY = pl.BlockSpec(memory_space=pl.ANY)
HBM = pl.BlockSpec(memory_space=pltpu.HBM)
VMEM = pl.BlockSpec(memory_space=pltpu.VMEM)
SMEM = pl.BlockSpec(memory_space=pltpu.SMEM)


def is_even():
    return lax.rem(lax.axis_index(AXIS), 2) == 0


class Order:
    def __init__(self):
        self.token = None

    def __call__(
        self, kernel, args, in_specs, out_shape, out_specs, scratch_shapes=(), weight=20e9, **kw
    ):
        places = {id(VMEM): pltpu.VMEM, id(HBM): pltpu.HBM}
        single = not isinstance(out_shape, list)
        out_shape = [out_shape] if single else out_shape
        out_specs = [out_specs] if single else out_specs
        args = [
            pltpu.with_memory_space_constraint(arg, places[id(spec)]) if id(spec) in places else arg
            for arg, spec in zip(args, in_specs)
        ]
        n_in, n_out, first = len(args), len(out_shape), self.token is None
        if not first:
            args = [*args, self.token]
            in_specs = [*in_specs, ANY]

        def without_tokens(*refs):
            rest = refs[len(args) :]
            kernel(*refs[:n_in], *rest[:n_out], *rest[n_out + 1 :])

        *outs, self.token = pl.pallas_call(
            without_tokens,
            out_shape=[*out_shape, pltpu.VMEM((8, 128), jnp.float32)],
            in_specs=in_specs,
            out_specs=[*out_specs, VMEM],
            scratch_shapes=scratch_shapes,
            compiler_params=pltpu.CompilerParams(vmem_limit_bytes=LIMIT),
            cost_estimate=pl.CostEstimate(flops=int(weight), bytes_accessed=0, transcendentals=0),
            **kw,
        )(*args)
        return outs[0] if single else outs


def inverse_norm(rows32):
    return 1.0 / jnp.sqrt(jnp.sum(rows32 * rows32, axis=1, keepdims=True) + 1e-06)


def unit(raw):
    rows32 = raw.astype(jnp.float32)
    return (rows32 * inverse_norm(rows32)).astype(jnp.bfloat16)


def tiles_of(size):
    return [pl.ds(start, min(TILE, size - start)) for start in range(0, size, TILE)]


def put_units(raw, out):
    for rows in tiles_of(ROWS):
        out[rows, :] = unit(raw[rows, :])


def put_labels(ids, out):
    out[ROWS:, :] = jnp.zeros((LABEL_ROWS, out.shape[1]), out.dtype)
    labels = jnp.broadcast_to(ids, (LABEL_ROWS, ROWS)).astype(jnp.float32)
    out[ROWS:, :ROWS] = labels.astype(out.dtype)


def line_of(block):
    return block[ROWS:, :].astype(jnp.float32)[:1, :ROWS]


def either(first_here, one, other):
    pl.when(first_here)(one)
    pl.when(jnp.logical_not(first_here))(other)


def part_copies(src, out, sems):
    part = ROWS // PARTS
    return [
        pltpu.make_async_copy(
            src.at[pl.ds(i * part, part)], out.at[pl.ds(i * part, part)], sems.at[i]
        )
        for i in range(PARTS)
    ]


def column_of(ids):
    lines = jnp.broadcast_to(ids, (8, ROWS)).astype(jnp.float32)
    return jnp.transpose(lines)[:, :1]


def own_kernel(
    images, texts, pair_ids, u_raw, v_raw, u, v, ids, labels, flat, flat_sem, u_sems, v_sems
):
    ids_copy = pltpu.make_async_copy(pair_ids, flat, flat_sem)
    ids_copy.start()

    def start(first, second):
        for copy in part_copies(first, u_raw, u_sems) + part_copies(second, v_raw, v_sems):
            copy.start()

    either(is_even(), lambda: start(images, texts), lambda: start(texts, images))
    ids_copy.wait()
    ids[...] = jnp.reshape(flat[...], ids.shape)
    labels[...] = column_of(ids[...])
    put_labels(ids[...], u)
    put_labels(ids[...], v)
    for copy in part_copies(images, u_raw, u_sems):
        copy.wait()
    put_units(u_raw, u)
    for copy in part_copies(texts, v_raw, v_sems):
        copy.wait()
    put_units(v_raw, v)


def own_blocks(call, images, texts, pair_ids):
    raw = pltpu.VMEM(images.shape, images.dtype)
    labelled = pltpu.VMEM((ROWS + LABEL_ROWS, images.shape[1]), images.dtype)
    return call(
        own_kernel,
        [images, texts, pair_ids],
        [HBM] * 3,
        [
            raw,
            raw,
            labelled,
            labelled,
            pltpu.VMEM((1, ROWS), pair_ids.dtype),
            pltpu.VMEM((ROWS, 1), jnp.float32),
        ],
        out_specs=[VMEM] * 6,
        scratch_shapes=[
            pltpu.VMEM(pair_ids.shape, pair_ids.dtype),
            pltpu.SemaphoreType.DMA,
            pltpu.SemaphoreType.DMA((PARTS,)),
            pltpu.SemaphoreType.DMA((PARTS,)),
        ],
        name="own_blocks",
    )


def neighbour_kernel(left_images, right_texts, ids, raw, out, labels):
    def take(src):
        for rows in tiles_of(ROWS):
            raw[rows, :] = src[rows, :]

    either(is_even(), lambda: take(left_images), lambda: take(right_texts))
    put_units(raw, out)
    put_labels(ids[...], out)
    labels[...] = column_of(ids[...])


def neighbour_block(call, left_images, right_texts, ids):
    width = left_images.shape[1]
    return call(
        neighbour_kernel,
        [left_images, right_texts, ids],
        [VMEM] * 3,
        [
            pltpu.VMEM((ROWS, width), left_images.dtype),
            pltpu.VMEM((ROWS + LABEL_ROWS, width), left_images.dtype),
            pltpu.VMEM((ROWS, 1), jnp.float32),
        ],
        out_specs=[VMEM] * 3,
        name="neighbour_block",
    )


def copy_kernel(*refs):
    half = len(refs) // 2
    for value, out in zip(refs[:half], refs[half:]):
        out[...] = value[...]


def copied(call, *values):
    return call(
        copy_kernel,
        values,
        [VMEM] * len(values),
        [pltpu.VMEM(value.shape, value.dtype) for value in values],
        out_specs=[VMEM] * len(values),
        name="copied",
        weight=W_COPIED,
    )


def contributions(log_scale, bias, labels_x, x, y, begin=0, end=ROWS):
    scale = jnp.exp(jnp.full((1, ROWS), log_scale[0], jnp.float32))
    rate = scale * -LOG2E
    shift = bias[0] * -LOG2E
    labels_y = line_of(y)
    tiles = [
        pl.ds(start, min(TILE, end - start)) for start in range(begin, end, TILE)
    ]

    def products(rows):
        return lax.dot_general(
            x[rows, :], y[:ROWS, :], (((1,), (1,)), ((), ())), preferred_element_type=jnp.float32
        )

    ahead = products(tiles[0])
    for i, rows in enumerate(tiles):
        now = ahead
        if i + 1 < len(tiles):
            ahead = products(tiles[i + 1])
        sigmoid = 1.0 / (1.0 + jnp.exp2(now * rate + shift))
        same = jnp.where(labels_x[rows, :] == labels_y, 1.0, 0.0)
        coef = ((sigmoid - same) * scale).astype(jnp.bfloat16)
        yield rows, jnp.dot(coef, y[:ROWS, :], preferred_element_type=jnp.float32)


def back_through(raw, grad):
    rows32 = raw.astype(jnp.float32)
    inverse = inverse_norm(rows32)
    exact = rows32 * inverse
    return (grad - exact * jnp.sum(exact * grad, axis=1, keepdims=True)) * inverse


def score_kernel(log_scale, bias, labels_x, x, y, *refs):
    out = refs[-1]
    for rows, grad in contributions(log_scale, bias, labels_x, x, y):
        out[rows, :] = refs[0][rows, :] + grad if len(refs) > 1 else grad


def score(call, scalars, labels_x, x, y, before=None):
    args = [*scalars, labels_x, x, y] + ([before] if before is not None else [])
    return call(
        score_kernel,
        args,
        [SMEM, SMEM] + [VMEM] * (len(args) - 2),
        pltpu.VMEM((ROWS, x.shape[1]), jnp.float32),
        out_specs=VMEM,
        input_output_aliases={5: 0} if before is not None else {},
        name="score",
    )


def close_kernel(log_scale, bias, labels_x, x, y, before, raw, out):
    for rows, grad in contributions(log_scale, bias, labels_x, x, y):
        out[rows, :] = back_through(raw[rows, :], before[rows, :] + grad)


def close(call, scalars, labels_x, x, y, before, raw):
    args = [*scalars, labels_x, x, y, before, raw]
    return call(
        close_kernel,
        args,
        [SMEM, SMEM] + [VMEM] * (len(args) - 2),
        pltpu.VMEM((ROWS, x.shape[1]), jnp.float32),
        out_specs=VMEM,
        input_output_aliases={5: 0},
        name="close",
        weight=W_CLOSE,
    )


def part_kernel(begin, log_scale, bias, labels_x, x, y, raw, *outs):
    end = begin + sum(out.shape[0] for out in outs)
    starts = [begin + sum(out.shape[0] for out in outs[:i]) for i in range(len(outs))]
    for rows, grad in contributions(log_scale, bias, labels_x, x, y, begin, end):
        result = back_through(raw[rows, :], grad).astype(outs[0].dtype)
        for out, start in zip(outs, starts):
            low, high = max(rows.start, start), min(rows.start + rows.size, start + out.shape[0])
            if low < high:
                out[low - start : high - start, :] = result[low - rows.start : high - rows.start]


def part(call, scalars, labels_x, x, y, raw, begin, sizes):
    return call(
        functools.partial(part_kernel, begin),
        [*scalars, labels_x, x, y, raw],
        [SMEM, SMEM, VMEM, VMEM, VMEM, VMEM],
        [pltpu.VMEM((size, x.shape[1]), x.dtype) for size in sizes],
        out_specs=[VMEM] * len(sizes),
        name="part",
    )


def finish_kernel(
    log_scale, bias, labels_x, x, y, before, raw, closed, image_grad, text_grad, sems
):
    copies = []
    for rows, grad in contributions(log_scale, bias, labels_x, x, y):
        closed[rows, :] = back_through(raw[rows, :], before[rows, :] + grad)
        image_copy, text_copy = [
            pltpu.make_async_copy(closed.at[rows], out.at[rows], sems.at[len(copies)])
            for out in (image_grad, text_grad)
        ]
        either(is_even(), image_copy.start, text_copy.start)
        copies.append(image_copy)
    for copy in copies:
        copy.wait()


def finish(call, scalars, labels_x, x, y, before, raw):
    shape = (ROWS, x.shape[1])
    _, *outs = call(
        finish_kernel,
        [*scalars, labels_x, x, y, before, raw],
        [SMEM, SMEM] + [VMEM] * 5,
        [pltpu.VMEM(shape, jnp.float32)] + [pltpu.HBM(shape, jnp.float32)] * 2,
        out_specs=[VMEM, HBM, HBM],
        input_output_aliases={5: 0},
        scratch_shapes=[pltpu.SemaphoreType.DMA((len(tiles_of(ROWS)),))],
        name="finish",
        weight=W_FINISH,
    )
    return outs


def add_kernel(begin, _image_grad, _text_grad, closed, piece, image_grad, text_grad, stage, sems):
    tiles = [pl.ds(start, ADD_TILE) for start in range(0, piece.shape[0], ADD_TILE)]

    def work(target):
        copies = []
        for rows in tiles:
            there = pl.ds(begin + rows.start, rows.size)
            stage[rows, :] = closed[there, :] + piece[rows, :].astype(jnp.float32)
            copies.append(
                pltpu.make_async_copy(stage.at[rows], target.at[there], sems.at[len(copies)])
            )
            copies[-1].start()
        for copy in copies:
            copy.wait()

    either(is_even(), lambda: work(text_grad), lambda: work(image_grad))


def add(call, closed, piece, outs, begin):
    size, width = piece.shape
    return call(
        functools.partial(add_kernel, begin),
        [*outs, closed, piece],
        [HBM, HBM, VMEM, VMEM],
        [pltpu.HBM((ROWS, width), jnp.float32)] * 2,
        out_specs=[HBM, HBM],
        input_output_aliases={0: 0, 1: 1},
        scratch_shapes=[
            pltpu.VMEM((size, width), jnp.float32),
            pltpu.SemaphoreType.DMA((size // ADD_TILE,)),
        ],
        name="add",
        weight=W_ADD,
    )


def pairs_of(even_step, odd_step):
    count = lax.axis_size(AXIS)
    return [(p, (p + (odd_step if p % 2 else even_step)) % count) for p in range(count)]


def permute(value, even_step, odd_step):
    return lax.ppermute(value, AXIS, pairs_of(even_step, odd_step))


def swap(value):
    return permute(value, 1, -1)


def across(value):
    return permute(value, -1, 1)


def on_device(images, texts, pair_ids, log_scale, bias):
    call = Order()
    scalars = (log_scale, bias)
    left_images = permute(images, 1, 1)
    right_texts = permute(texts, -1, -1)

    u_raw, v_raw, u, v, ids, labels = own_blocks(call, images, texts, pair_ids)
    grad_u = score(call, scalars, labels, u, v)
    grad_v = score(call, scalars, labels, v, u)
    u_again, ids_again = copied(call, u, ids)
    y = permute(u_again, 3, -3)
    s0 = swap(u_again)
    near_ids = across(ids_again)

    x_raw, x, near_labels = neighbour_block(call, left_images, right_texts, near_ids)
    s1 = swap(x)
    grad_u = score(call, scalars, labels, u, s0, grad_u)
    early, late = part(call, scalars, near_labels, x, s1, x_raw, 0, PIECES)
    early, late = across(early), across(late)
    grad_v = score(call, scalars, labels, v, x, grad_v)
    grad_u = score(call, scalars, labels, u, s1, grad_u)

    s2 = swap(*copied(call, y))
    outs = finish(call, scalars, labels, u, y, grad_u, u_raw)
    closed = close(call, scalars, labels, v, s2, grad_v, v_raw)
    outs = add(call, closed, early, outs, 0)
    return tuple(add(call, closed, late, outs, PIECES[0]))


def solution(mesh):
    in_specs = (P("dp", None), P("dp", None), P("dp"), P(), P())
    out_specs = (P("dp", None), P("dp", None))
    return jax.shard_map(
        on_device, mesh=mesh, in_specs=in_specs, out_specs=out_specs, check_vma=False
    )
```

```python
import functools

import jax
import jax.numpy as jnp
from jax import lax
from jax.experimental import pallas as pl
from jax.experimental.pallas import tpu as pltpu
from jax.sharding import PartitionSpec as P

AXIS = "dp"
TILE = 256
ROWS = 768
LABEL_ROWS = 16
PIECES = (352, 416)
PARTS = 4
ADD_TILE = 32
LIMIT = 16 * 1024 * 1024
W_CLOSE = 20e9
W_COPIED = 20e9
W_ADD = 20e9
LOG2E = 1.4426950408889634
ANY = pl.BlockSpec(memory_space=pl.ANY)
HBM = pl.BlockSpec(memory_space=pltpu.HBM)
VMEM = pl.BlockSpec(memory_space=pltpu.VMEM)
SMEM = pl.BlockSpec(memory_space=pltpu.SMEM)


def is_even():
    return lax.rem(lax.axis_index(AXIS), 2) == 0


class Order:
    def __init__(self):
        self.token = None

    def __call__(
        self, kernel, args, in_specs, out_shape, out_specs, scratch_shapes=(), weight=20e9, **kw
    ):
        places = {id(VMEM): pltpu.VMEM, id(HBM): pltpu.HBM}
        single = not isinstance(out_shape, list)
        out_shape = [out_shape] if single else out_shape
        out_specs = [out_specs] if single else out_specs
        args = [
            pltpu.with_memory_space_constraint(arg, places[id(spec)]) if id(spec) in places else arg
            for arg, spec in zip(args, in_specs)
        ]
        n_in, n_out, first = len(args), len(out_shape), self.token is None
        if not first:
            args = [*args, self.token]
            in_specs = [*in_specs, ANY]

        def without_tokens(*refs):
            rest = refs[len(args) :]
            kernel(*refs[:n_in], *rest[:n_out], *rest[n_out + 1 :])

        *outs, self.token = pl.pallas_call(
            without_tokens,
            out_shape=[*out_shape, pltpu.VMEM((8, 128), jnp.float32)],
            in_specs=in_specs,
            out_specs=[*out_specs, VMEM],
            scratch_shapes=scratch_shapes,
            compiler_params=pltpu.CompilerParams(vmem_limit_bytes=LIMIT),
            cost_estimate=pl.CostEstimate(flops=int(weight), bytes_accessed=0, transcendentals=0),
            **kw,
        )(*args)
        return outs[0] if single else outs


def inverse_norm(rows32):
    return 1.0 / jnp.sqrt(jnp.sum(rows32 * rows32, axis=1, keepdims=True) + 1e-06)


def unit(raw):
    rows32 = raw.astype(jnp.float32)
    return (rows32 * inverse_norm(rows32)).astype(jnp.bfloat16)


def tiles_of(size):
    return [pl.ds(start, min(TILE, size - start)) for start in range(0, size, TILE)]


def put_units(raw, out):
    for rows in tiles_of(ROWS):
        out[rows, :] = unit(raw[rows, :])


def put_labels(ids, out):
    out[ROWS:, :] = jnp.zeros((LABEL_ROWS, out.shape[1]), out.dtype)
    labels = jnp.broadcast_to(ids, (LABEL_ROWS, ROWS)).astype(jnp.float32)
    out[ROWS:, :ROWS] = labels.astype(out.dtype)


def line_of(block):
    return block[ROWS:, :].astype(jnp.float32)[:1, :ROWS]


def either(first_here, one, other):
    pl.when(first_here)(one)
    pl.when(jnp.logical_not(first_here))(other)


def part_copies(src, out, sems):
    part = ROWS // PARTS
    return [
        pltpu.make_async_copy(
            src.at[pl.ds(i * part, part)], out.at[pl.ds(i * part, part)], sems.at[i]
        )
        for i in range(PARTS)
    ]


def column_of(ids):
    lines = jnp.broadcast_to(ids, (8, ROWS)).astype(jnp.float32)
    return jnp.transpose(lines)[:, :1]


def own_kernel(
    images, texts, pair_ids, u_raw, v_raw, u, v, ids, labels, flat, flat_sem, u_sems, v_sems
):
    ids_copy = pltpu.make_async_copy(pair_ids, flat, flat_sem)
    ids_copy.start()

    def start(first, second):
        for copy in part_copies(first, u_raw, u_sems) + part_copies(second, v_raw, v_sems):
            copy.start()

    either(is_even(), lambda: start(images, texts), lambda: start(texts, images))
    ids_copy.wait()
    ids[...] = jnp.reshape(flat[...], ids.shape)
    labels[...] = column_of(ids[...])
    put_labels(ids[...], u)
    put_labels(ids[...], v)
    for copy in part_copies(images, u_raw, u_sems):
        copy.wait()
    put_units(u_raw, u)
    for copy in part_copies(texts, v_raw, v_sems):
        copy.wait()
    put_units(v_raw, v)


def own_blocks(call, images, texts, pair_ids):
    raw = pltpu.VMEM(images.shape, images.dtype)
    labelled = pltpu.VMEM((ROWS + LABEL_ROWS, images.shape[1]), images.dtype)
    return call(
        own_kernel,
        [images, texts, pair_ids],
        [HBM] * 3,
        [
            raw,
            raw,
            labelled,
            labelled,
            pltpu.VMEM((1, ROWS), pair_ids.dtype),
            pltpu.VMEM((ROWS, 1), jnp.float32),
        ],
        out_specs=[VMEM] * 6,
        scratch_shapes=[
            pltpu.VMEM(pair_ids.shape, pair_ids.dtype),
            pltpu.SemaphoreType.DMA,
            pltpu.SemaphoreType.DMA((PARTS,)),
            pltpu.SemaphoreType.DMA((PARTS,)),
        ],
        name="own_blocks",
    )


def neighbour_kernel(left_images, right_texts, ids, raw, out, labels):
    def take(src):
        for rows in tiles_of(ROWS):
            raw[rows, :] = src[rows, :]

    either(is_even(), lambda: take(left_images), lambda: take(right_texts))
    put_units(raw, out)
    put_labels(ids[...], out)
    labels[...] = column_of(ids[...])


def neighbour_block(call, left_images, right_texts, ids):
    width = left_images.shape[1]
    return call(
        neighbour_kernel,
        [left_images, right_texts, ids],
        [VMEM] * 3,
        [
            pltpu.VMEM((ROWS, width), left_images.dtype),
            pltpu.VMEM((ROWS + LABEL_ROWS, width), left_images.dtype),
            pltpu.VMEM((ROWS, 1), jnp.float32),
        ],
        out_specs=[VMEM] * 3,
        name="neighbour_block",
    )


def copy_kernel(*refs):
    half = len(refs) // 2
    for value, out in zip(refs[:half], refs[half:]):
        out[...] = value[...]


def copied(call, *values):
    return call(
        copy_kernel,
        values,
        [VMEM] * len(values),
        [pltpu.VMEM(value.shape, value.dtype) for value in values],
        out_specs=[VMEM] * len(values),
        name="copied",
        weight=W_COPIED,
    )


def contributions(log_scale, bias, labels_x, x, y, begin=0, end=ROWS):
    scale = jnp.exp(jnp.full((1, ROWS), log_scale[0], jnp.float32))
    rate = scale * -LOG2E
    shift = bias[0] * -LOG2E
    labels_y = line_of(y)
    tiles = [
        pl.ds(start, min(TILE, end - start)) for start in range(begin, end, TILE)
    ]

    def products(rows):
        return lax.dot_general(
            x[rows, :], y[:ROWS, :], (((1,), (1,)), ((), ())), preferred_element_type=jnp.float32
        )

    ahead = products(tiles[0])
    for i, rows in enumerate(tiles):
        now = ahead
        if i + 1 < len(tiles):
            ahead = products(tiles[i + 1])
        sigmoid = 1.0 / (1.0 + jnp.exp2(now * rate + shift))
        same = jnp.where(labels_x[rows, :] == labels_y, 1.0, 0.0)
        coef = ((sigmoid - same) * scale).astype(jnp.bfloat16)
        yield rows, jnp.dot(coef, y[:ROWS, :], preferred_element_type=jnp.float32)


def back_through(raw, grad):
    rows32 = raw.astype(jnp.float32)
    inverse = inverse_norm(rows32)
    exact = rows32 * inverse
    return (grad - exact * jnp.sum(exact * grad, axis=1, keepdims=True)) * inverse


def score_kernel(log_scale, bias, labels_x, x, y, *refs):
    out = refs[-1]
    for rows, grad in contributions(log_scale, bias, labels_x, x, y):
        out[rows, :] = refs[0][rows, :] + grad if len(refs) > 1 else grad


def score(call, scalars, labels_x, x, y, before=None):
    args = [*scalars, labels_x, x, y] + ([before] if before is not None else [])
    return call(
        score_kernel,
        args,
        [SMEM, SMEM] + [VMEM] * (len(args) - 2),
        pltpu.VMEM((ROWS, x.shape[1]), jnp.float32),
        out_specs=VMEM,
        input_output_aliases={5: 0} if before is not None else {},
        name="score",
    )


def close_kernel(log_scale, bias, labels_x, x, y, before, raw, out, *_):
    for rows, grad in contributions(log_scale, bias, labels_x, x, y):
        out[rows, :] = back_through(raw[rows, :], before[rows, :] + grad)


def close(call, scalars, labels_x, x, y, before, raw):
    shape = (ROWS, x.shape[1])
    closed, *outs = call(
        close_kernel,
        [*scalars, labels_x, x, y, before, raw],
        [SMEM, SMEM] + [VMEM] * 5,
        [pltpu.VMEM(shape, jnp.float32)] + [pltpu.HBM(shape, jnp.float32)] * 2,
        out_specs=[VMEM, HBM, HBM],
        input_output_aliases={5: 0},
        name="close",
        weight=W_CLOSE,
    )
    return closed, outs


def close_and_store_kernel(
    log_scale, bias, labels_x, x, y, before, raw, ready, _image_grad, _text_grad, out, image_grad, text_grad, sems
):
    image_copies = part_copies(ready, image_grad, sems)
    text_copies = part_copies(ready, text_grad, sems)

    def start(copies):
        for copy in copies:
            copy.start()

    either(is_even(), lambda: start(image_copies), lambda: start(text_copies))
    close_kernel(log_scale, bias, labels_x, x, y, before, raw, out)
    for copy in image_copies:
        copy.wait()


def close_and_store(call, scalars, labels_x, x, y, before, raw, ready, outs):
    shape = (ROWS, x.shape[1])
    closed, *outs = call(
        close_and_store_kernel,
        [*scalars, labels_x, x, y, before, raw, ready, *outs],
        [SMEM, SMEM] + [VMEM] * 6 + [HBM] * 2,
        [pltpu.VMEM(shape, jnp.float32)] + [pltpu.HBM(shape, jnp.float32)] * 2,
        out_specs=[VMEM, HBM, HBM],
        input_output_aliases={5: 0, 8: 1, 9: 2},
        scratch_shapes=[pltpu.SemaphoreType.DMA((PARTS,))],
        name="close",
        weight=W_CLOSE,
    )
    return closed, outs


def part_kernel(begin, log_scale, bias, labels_x, x, y, raw, *outs):
    end = begin + sum(out.shape[0] for out in outs)
    starts = [begin + sum(out.shape[0] for out in outs[:i]) for i in range(len(outs))]
    for rows, grad in contributions(log_scale, bias, labels_x, x, y, begin, end):
        result = back_through(raw[rows, :], grad).astype(outs[0].dtype)
        for out, start in zip(outs, starts):
            low, high = max(rows.start, start), min(rows.start + rows.size, start + out.shape[0])
            if low < high:
                out[low - start : high - start, :] = result[low - rows.start : high - rows.start]


def part(call, scalars, labels_x, x, y, raw, begin, sizes):
    return call(
        functools.partial(part_kernel, begin),
        [*scalars, labels_x, x, y, raw],
        [SMEM, SMEM, VMEM, VMEM, VMEM, VMEM],
        [pltpu.VMEM((size, x.shape[1]), x.dtype) for size in sizes],
        out_specs=[VMEM] * len(sizes),
        name="part",
    )


def growing(rows):
    sizes, start = [], 0
    while start < rows:
        size = min(ADD_TILE << len(sizes), rows - start)
        sizes.append((start, size))
        start += size
    return sizes


def add_kernel(begin, on, _image_grad, _text_grad, closed, piece, image_grad, text_grad, stage, sems):
    tiles = [pl.ds(start, size) for start, size in growing(piece.shape[0])]

    def work(target):
        copies = []
        for rows in tiles:
            there = pl.ds(begin + rows.start, rows.size)
            stage[rows, :] = closed[there, :] + piece[rows, :].astype(jnp.float32)
            copies.append(
                pltpu.make_async_copy(stage.at[rows], target.at[there], sems.at[len(copies)])
            )
            copies[-1].start()
        for copy in copies:
            copy.wait()

    if "even" in on:
        pl.when(is_even())(lambda: work(text_grad))
    if "odd" in on:
        pl.when(jnp.logical_not(is_even()))(lambda: work(image_grad))


def add(call, closed, piece, outs, begin, on=("even", "odd")):
    size, width = piece.shape
    return call(
        functools.partial(add_kernel, begin, on),
        [*outs, closed, piece],
        [HBM, HBM, VMEM, VMEM],
        [pltpu.HBM((ROWS, width), jnp.float32)] * 2,
        out_specs=[HBM, HBM],
        input_output_aliases={0: 0, 1: 1},
        scratch_shapes=[
            pltpu.VMEM((size, width), jnp.float32),
            pltpu.SemaphoreType.DMA((len(growing(size)),)),
        ],
        name="add",
        weight=W_ADD,
    )


def pairs_of(even_step, odd_step):
    count = lax.axis_size(AXIS)
    return [(p, (p + (odd_step if p % 2 else even_step)) % count) for p in range(count)]


def permute(value, even_step, odd_step):
    return lax.ppermute(value, AXIS, pairs_of(even_step, odd_step))


def swap(value):
    return permute(value, 1, -1)


def across(value):
    return permute(value, -1, 1)


def on_device(images, texts, pair_ids, log_scale, bias):
    call = Order()
    scalars = (log_scale, bias)
    left_images = permute(images, 1, 1)
    right_texts = permute(texts, -1, -1)

    u_raw, v_raw, u, v, ids, labels = own_blocks(call, images, texts, pair_ids)
    grad_u = score(call, scalars, labels, u, v)
    grad_v = score(call, scalars, labels, v, u)
    u_again, ids_again = copied(call, u, ids)
    y = permute(u_again, 3, -3)
    s0 = swap(u_again)
    near_ids = across(ids_again)

    x_raw, x, near_labels = neighbour_block(call, left_images, right_texts, near_ids)
    s1 = swap(x)
    grad_u = score(call, scalars, labels, u, s0, grad_u)
    early, late = part(call, scalars, near_labels, x, s1, x_raw, 0, PIECES)
    early = across(early)
    late = across(late)
    grad_v = score(call, scalars, labels, v, x, grad_v)
    grad_u = score(call, scalars, labels, u, s1, grad_u)

    s2 = swap(*copied(call, y))
    ready, outs = close(call, scalars, labels, u, y, grad_u, u_raw)
    closed, outs = close_and_store(call, scalars, labels, v, s2, grad_v, v_raw, ready, outs)
    outs = add(call, closed, early, outs, 0)
    return tuple(add(call, closed, late, outs, PIECES[0]))


def solution(mesh):
    in_specs = (P("dp", None), P("dp", None), P("dp"), P(), P())
    out_specs = (P("dp", None), P("dp", None))
    return jax.shard_map(
        on_device, mesh=mesh, in_specs=in_specs, out_specs=out_specs, check_vma=False
    )
```

```python
import functools

import jax
import jax.numpy as jnp
from jax import lax
from jax.experimental import pallas as pl
from jax.experimental.pallas import tpu as pltpu
from jax.sharding import PartitionSpec as P

AXIS = "dp"
TILE = 256
ROWS = 768
LABEL_ROWS = 16
PIECES = (368, 400)
PARTS = 4
ADD_TILE = 32
STRIP = 16
LIMIT = 16 * 1024 * 1024
W_CLOSE = 20e9
W_COPIED = 20e9
W_ADD = 20e9
LOG2E = 1.4426950408889634
ANY = pl.BlockSpec(memory_space=pl.ANY)
HBM = pl.BlockSpec(memory_space=pltpu.HBM)
VMEM = pl.BlockSpec(memory_space=pltpu.VMEM)
SMEM = pl.BlockSpec(memory_space=pltpu.SMEM)


def is_even():
    return lax.rem(lax.axis_index(AXIS), 2) == 0


class Order:
    def __init__(self):
        self.token = None

    def __call__(
        self, kernel, args, in_specs, out_shape, out_specs, scratch_shapes=(), weight=20e9, **kw
    ):
        places = {id(VMEM): pltpu.VMEM, id(HBM): pltpu.HBM}
        single = not isinstance(out_shape, list)
        out_shape = [out_shape] if single else out_shape
        out_specs = [out_specs] if single else out_specs
        args = [
            pltpu.with_memory_space_constraint(arg, places[id(spec)]) if id(spec) in places else arg
            for arg, spec in zip(args, in_specs)
        ]
        n_in, n_out, first = len(args), len(out_shape), self.token is None
        if not first:
            args = [*args, self.token]
            in_specs = [*in_specs, ANY]

        def without_tokens(*refs):
            rest = refs[len(args) :]
            kernel(*refs[:n_in], *rest[:n_out], *rest[n_out + 1 :])

        *outs, self.token = pl.pallas_call(
            without_tokens,
            out_shape=[*out_shape, pltpu.VMEM((8, 128), jnp.float32)],
            in_specs=in_specs,
            out_specs=[*out_specs, VMEM],
            scratch_shapes=scratch_shapes,
            compiler_params=pltpu.CompilerParams(vmem_limit_bytes=LIMIT),
            cost_estimate=pl.CostEstimate(flops=int(weight), bytes_accessed=0, transcendentals=0),
            **kw,
        )(*args)
        return outs[0] if single else outs


def inverse_norm(rows32):
    return 1.0 / jnp.sqrt(jnp.sum(rows32 * rows32, axis=1, keepdims=True) + 1e-06)


def unit(raw):
    rows32 = raw.astype(jnp.float32)
    return (rows32 * inverse_norm(rows32)).astype(jnp.bfloat16)


def tiles_of(size):
    return [pl.ds(start, min(TILE, size - start)) for start in range(0, size, TILE)]


def put_units(raw, out):
    for rows in tiles_of(ROWS):
        out[rows, :] = unit(raw[rows, :])


def put_labels(ids, out):
    out[ROWS:, :] = jnp.zeros((LABEL_ROWS, out.shape[1]), out.dtype)
    labels = jnp.broadcast_to(ids, (LABEL_ROWS, ROWS)).astype(jnp.float32)
    out[ROWS:, :ROWS] = labels.astype(out.dtype)


def line_of(block):
    return block[ROWS:, :].astype(jnp.float32)[:1, :ROWS]


def either(first_here, one, other):
    pl.when(first_here)(one)
    pl.when(jnp.logical_not(first_here))(other)


def part_copies(src, out, sems):
    part = ROWS // PARTS
    return [
        pltpu.make_async_copy(
            src.at[pl.ds(i * part, part)], out.at[pl.ds(i * part, part)], sems.at[i]
        )
        for i in range(PARTS)
    ]


def column_of(ids):
    lines = jnp.broadcast_to(ids, (8, ROWS)).astype(jnp.float32)
    return jnp.transpose(lines)[:, :1]


def own_kernel(
    images, texts, pair_ids, u_raw, v_raw, u, v, ids, labels, flat, flat_sem, u_sems, v_sems
):
    ids_copy = pltpu.make_async_copy(pair_ids, flat, flat_sem)
    ids_copy.start()

    def start(first, second):
        for copy in part_copies(first, u_raw, u_sems) + part_copies(second, v_raw, v_sems):
            copy.start()

    either(is_even(), lambda: start(images, texts), lambda: start(texts, images))
    ids_copy.wait()
    ids[...] = jnp.reshape(flat[...], ids.shape)
    labels[...] = column_of(ids[...])
    put_labels(ids[...], u)
    put_labels(ids[...], v)
    for copy in part_copies(images, u_raw, u_sems):
        copy.wait()
    put_units(u_raw, u)
    for copy in part_copies(texts, v_raw, v_sems):
        copy.wait()
    put_units(v_raw, v)


def own_blocks(call, images, texts, pair_ids):
    raw = pltpu.VMEM(images.shape, images.dtype)
    labelled = pltpu.VMEM((ROWS + LABEL_ROWS, images.shape[1]), images.dtype)
    return call(
        own_kernel,
        [images, texts, pair_ids],
        [HBM] * 3,
        [
            raw,
            raw,
            labelled,
            labelled,
            pltpu.VMEM((1, ROWS), pair_ids.dtype),
            pltpu.VMEM((ROWS, 1), jnp.float32),
        ],
        out_specs=[VMEM] * 6,
        scratch_shapes=[
            pltpu.VMEM(pair_ids.shape, pair_ids.dtype),
            pltpu.SemaphoreType.DMA,
            pltpu.SemaphoreType.DMA((PARTS,)),
            pltpu.SemaphoreType.DMA((PARTS,)),
        ],
        name="own_blocks",
    )


def neighbour_kernel(left_images, right_texts, ids, raw, out, labels):
    def take(src):
        for rows in tiles_of(ROWS):
            raw[rows, :] = src[rows, :]

    either(is_even(), lambda: take(left_images), lambda: take(right_texts))
    put_units(raw, out)
    put_labels(ids[...], out)
    labels[...] = column_of(ids[...])


def neighbour_block(call, left_images, right_texts, ids):
    width = left_images.shape[1]
    return call(
        neighbour_kernel,
        [left_images, right_texts, ids],
        [VMEM] * 3,
        [
            pltpu.VMEM((ROWS, width), left_images.dtype),
            pltpu.VMEM((ROWS + LABEL_ROWS, width), left_images.dtype),
            pltpu.VMEM((ROWS, 1), jnp.float32),
        ],
        out_specs=[VMEM] * 3,
        name="neighbour_block",
    )


def copy_kernel(*refs):
    half = len(refs) // 2
    for value, out in zip(refs[:half], refs[half:]):
        out[...] = value[...]


def copied(call, *values):
    return call(
        copy_kernel,
        values,
        [VMEM] * len(values),
        [pltpu.VMEM(value.shape, value.dtype) for value in values],
        out_specs=[VMEM] * len(values),
        name="copied",
        weight=W_COPIED,
    )


def contributions(log_scale, bias, labels_x, x, y, begin=0, end=ROWS):
    scale = jnp.exp(jnp.full((1, ROWS), log_scale[0], jnp.float32))
    rate = scale * -LOG2E
    shift = bias[0] * -LOG2E
    labels_y = line_of(y)
    tiles = [
        pl.ds(start, min(TILE, end - start)) for start in range(begin, end, TILE)
    ]

    def products(rows):
        return lax.dot_general(
            x[rows, :], y[:ROWS, :], (((1,), (1,)), ((), ())), preferred_element_type=jnp.float32
        )

    ahead = products(tiles[0])
    for i, rows in enumerate(tiles):
        now = ahead
        if i + 1 < len(tiles):
            ahead = products(tiles[i + 1])
        sigmoid = 1.0 / (1.0 + jnp.exp2(now * rate + shift))
        same = jnp.where(labels_x[rows, :] == labels_y, 1.0, 0.0)
        coef = ((sigmoid - same) * scale).astype(jnp.bfloat16)
        yield rows, jnp.dot(coef, y[:ROWS, :], preferred_element_type=jnp.float32)


def back_through(raw, grad):
    rows32 = raw.astype(jnp.float32)
    inverse = inverse_norm(rows32)
    exact = rows32 * inverse
    return (grad - exact * jnp.sum(exact * grad, axis=1, keepdims=True)) * inverse


def score_kernel(log_scale, bias, labels_x, x, y, *refs):
    out = refs[-1]
    for rows, grad in contributions(log_scale, bias, labels_x, x, y):
        out[rows, :] = refs[0][rows, :] + grad if len(refs) > 1 else grad


def score(call, scalars, labels_x, x, y, before=None):
    args = [*scalars, labels_x, x, y] + ([before] if before is not None else [])
    return call(
        score_kernel,
        args,
        [SMEM, SMEM] + [VMEM] * (len(args) - 2),
        pltpu.VMEM((ROWS, x.shape[1]), jnp.float32),
        out_specs=VMEM,
        input_output_aliases={5: 0} if before is not None else {},
        name="score",
    )


def close_kernel(log_scale, bias, labels_x, x, y, before, raw, out, *_):
    for rows, grad in contributions(log_scale, bias, labels_x, x, y):
        out[rows, :] = back_through(raw[rows, :], before[rows, :] + grad)


def close(call, scalars, labels_x, x, y, before, raw):
    shape = (ROWS, x.shape[1])
    closed, *outs = call(
        close_kernel,
        [*scalars, labels_x, x, y, before, raw],
        [SMEM, SMEM] + [VMEM] * 5,
        [pltpu.VMEM(shape, jnp.float32)] + [pltpu.HBM(shape, jnp.float32)] * 2,
        out_specs=[VMEM, HBM, HBM],
        input_output_aliases={5: 0},
        name="close",
        weight=W_CLOSE,
    )
    return closed, outs


def close_and_store_kernel(
    log_scale, bias, labels_x, x, y, before, raw, ready, _image_grad, _text_grad, out, image_grad, text_grad, sems
):
    image_copies = part_copies(ready, image_grad, sems)
    text_copies = part_copies(ready, text_grad, sems)

    def start(copies):
        for copy in copies:
            copy.start()

    either(is_even(), lambda: start(image_copies), lambda: start(text_copies))
    close_kernel(log_scale, bias, labels_x, x, y, before, raw, out)
    for copy in image_copies:
        copy.wait()


def close_and_store(call, scalars, labels_x, x, y, before, raw, ready, outs):
    shape = (ROWS, x.shape[1])
    closed, *outs = call(
        close_and_store_kernel,
        [*scalars, labels_x, x, y, before, raw, ready, *outs],
        [SMEM, SMEM] + [VMEM] * 6 + [HBM] * 2,
        [pltpu.VMEM(shape, jnp.float32)] + [pltpu.HBM(shape, jnp.float32)] * 2,
        out_specs=[VMEM, HBM, HBM],
        input_output_aliases={5: 0, 8: 1, 9: 2},
        scratch_shapes=[pltpu.SemaphoreType.DMA((PARTS,))],
        name="close",
        weight=W_CLOSE,
    )
    return closed, outs


def part_kernel(begin, log_scale, bias, labels_x, x, y, raw, *outs):
    end = begin + sum(out.shape[0] for out in outs)
    starts = [begin + sum(out.shape[0] for out in outs[:i]) for i in range(len(outs))]
    for rows, grad in contributions(log_scale, bias, labels_x, x, y, begin, end):
        result = back_through(raw[rows, :], grad).astype(outs[0].dtype)
        for out, start in zip(outs, starts):
            low, high = max(rows.start, start), min(rows.start + rows.size, start + out.shape[0])
            if low < high:
                out[low - start : high - start, :] = result[low - rows.start : high - rows.start]


def part(call, scalars, labels_x, x, y, raw, begin, sizes):
    return call(
        functools.partial(part_kernel, begin),
        [*scalars, labels_x, x, y, raw],
        [SMEM, SMEM, VMEM, VMEM, VMEM, VMEM],
        [pltpu.VMEM((size, x.shape[1]), x.dtype) for size in sizes],
        out_specs=[VMEM] * len(sizes),
        name="part",
    )


def growing(rows):
    sizes, start = [], 0
    while start < rows:
        size = min(ADD_TILE << len(sizes), rows - start)
        sizes.append((start, size))
        start += size
    return sizes


def add_kernel(begin, _image_grad, _text_grad, closed, piece, image_grad, text_grad, stage, sems):
    copies = []
    for start, size in growing(piece.shape[0]):

        @pl.loop(start // STRIP, (start + size) // STRIP)
        def _(i):
            at = pl.multiple_of(i * STRIP, STRIP)
            rows, there = pl.ds(at, STRIP), pl.ds(pl.multiple_of(begin + at, STRIP), STRIP)
            stage[rows, :] = closed[there, :] + piece[rows, :].astype(jnp.float32)

        rows, there = pl.ds(start, size), pl.ds(begin + start, size)
        image_copy, text_copy = [
            pltpu.make_async_copy(stage.at[rows], out.at[there], sems.at[len(copies)])
            for out in (image_grad, text_grad)
        ]
        either(is_even(), text_copy.start, image_copy.start)
        copies.append(image_copy)
    for copy in copies:
        copy.wait()


def add(call, closed, piece, outs, begin):
    size, width = piece.shape
    return call(
        functools.partial(add_kernel, begin),
        [*outs, closed, piece],
        [HBM, HBM, VMEM, VMEM],
        [pltpu.HBM((ROWS, width), jnp.float32)] * 2,
        out_specs=[HBM, HBM],
        input_output_aliases={0: 0, 1: 1},
        scratch_shapes=[
            pltpu.VMEM((size, width), jnp.float32),
            pltpu.SemaphoreType.DMA((len(growing(size)),)),
        ],
        name="add",
        weight=W_ADD,
    )


def pairs_of(even_step, odd_step):
    count = lax.axis_size(AXIS)
    return [(p, (p + (odd_step if p % 2 else even_step)) % count) for p in range(count)]


def permute(value, even_step, odd_step):
    return lax.ppermute(value, AXIS, pairs_of(even_step, odd_step))


def swap(value):
    return permute(value, 1, -1)


def across(value):
    return permute(value, -1, 1)


def on_device(images, texts, pair_ids, log_scale, bias):
    call = Order()
    scalars = (log_scale, bias)
    left_images = permute(images, 1, 1)
    right_texts = permute(texts, -1, -1)

    u_raw, v_raw, u, v, ids, labels = own_blocks(call, images, texts, pair_ids)
    grad_u = score(call, scalars, labels, u, v)
    grad_v = score(call, scalars, labels, v, u)
    u_again, ids_again = copied(call, u, ids)
    y = permute(u_again, 3, -3)
    s0 = swap(u_again)
    near_ids = across(ids_again)

    x_raw, x, near_labels = neighbour_block(call, left_images, right_texts, near_ids)
    s1 = swap(x)
    grad_u = score(call, scalars, labels, u, s0, grad_u)
    early, late = part(call, scalars, near_labels, x, s1, x_raw, 0, PIECES)
    early = across(early)
    late = across(late)
    grad_v = score(call, scalars, labels, v, x, grad_v)
    grad_u = score(call, scalars, labels, u, s1, grad_u)

    s2 = swap(*copied(call, y))
    ready, outs = close(call, scalars, labels, u, y, grad_u, u_raw)
    closed, outs = close_and_store(call, scalars, labels, v, s2, grad_v, v_raw, ready, outs)
    outs = add(call, closed, early, outs, 0)
    return tuple(add(call, closed, late, outs, PIECES[0]))


def solution(mesh):
    in_specs = (P("dp", None), P("dp", None), P("dp"), P(), P())
    out_specs = (P("dp", None), P("dp", None))
    return jax.shard_map(
        on_device, mesh=mesh, in_specs=in_specs, out_specs=out_specs, check_vma=False
    )
```
